512 devices in a mesh: batch: 32 (over x, z), tensor: 16 (over y, core).
Axes of the slice: x: 4, y: 8, z: 8, core: 2. Of those that a mesh axis runs over, the one named last changes fastest.
Arguments:
- queries: bfloat16 [512, 4, 16384], P('batch', None, 'tensor'), may hold values from -8 to 8
- new_kv: bfloat16 [512, 4, 4096], P('batch', None, 'tensor'), may hold values from -6 to 6
- resident_pages: bfloat16 [2688, 64, 4096], P('batch', None, 'tensor'), may hold values from -6 to 6
- arriving_pages: bfloat16 [896, 64, 2048], P('batch', 'tensor'), may hold values from -6 to 6
- block_table: int32 [384, 7], P('batch'), may hold values from 0 to 83, as said below
- old_lengths: int32 [384], P('batch'), may hold values from 1 to 448, as said below
- new_slots: int32 [128], P('batch'), may hold values from 0 to 15, as said below
- page_owner: int32 [896], replicated, may hold values from 0 to 31, as said below
- page_position: int32 [896], replicated, may hold values from 0 to 27, as said below
- page_tokens: int32 [896], replicated, may hold values from 0 to 64, as said below
Outputs:
- attention_out: bfloat16 [512, 4, 16384], P('batch', None, 'tensor')
- arrived_pages: bfloat16 [896, 64, 4096], P('batch', None, 'tensor')
The draws below stay inside these ranges and needn't reach their ends.
Inputs may be any that keep to these rules, and one draw needn't show every extreme that they name: `block_table`: the rows of one decode group's resident requests name every one of its 84 resident pages exactly once. `old_lengths`: in every decode group one resident request has 448 cached tokens. `new_slots`: within one decode group the slots are distinct and increasing. `page_owner`: every decode group receives exactly 28 arriving pages; one prefill owner sends at most 2 pages to one decode group, and exactly 2 to some. `page_position`: the places of one decode group's arriving pages are distinct; places k * 7 to k * 7 + 6 hold new request k's pages in order. `page_tokens`: A new request of L tokens has min(max(L - i * 64, 0), 64) valid tokens in its page i, and L is at least 1; some new request has 448 tokens.
All inputs are finite; a program needn't handle non-finite values.
Results may differ from the reference program's by a relative error of at most 0.0031.
Values may be sent and summed in bfloat16 or wider, within the bound.
A program may use at most 64 MiB of HBM per device.

```python
import math
import jax
import jax.numpy as jnp
from jax import lax

HD = 128
HQ = 128
KV_HEADS = 8
PAGE = 64
P_SIZE = 7
STEPS = 4
NEW_DEV = 4
REQ_DEV = 16
OLD_DEV = 12
APD = 28
CAP = 2
POOL = 84
KV_COPIES = 16
REQUESTS = 512
N_BATCH = 32


def shuffled_rows(key, count, length):
    keys = jax.random.split(key, count)
    return jax.vmap(partial_permutation, in_axes=(0, None))(keys, length)


def partial_permutation(key, length):
    return jax.random.permutation(key, length)


def arrival_plan(key):
    inner = jax.random.fold_in(key, 61)
    key_offsets, key_shuffle, key_places, key_lengths, key_spot = jax.random.split(inner, 5)
    units = (APD + CAP - 1) // CAP
    candidates = jnp.arange(N_BATCH, dtype=jnp.int32)
    priority = jax.random.permutation(key_offsets, N_BATCH).astype(jnp.int32)
    priority = jnp.where(candidates == 1, -2, jnp.where(candidates == N_BATCH // 2, -1, priority))
    offsets = jnp.argsort(priority)[:units].astype(jnp.int32)
    pattern = offsets[jnp.arange(APD) % units]
    shuffle = shuffled_rows(key_shuffle, N_BATCH, APD)
    owners = (jnp.arange(N_BATCH)[:, None] + pattern[shuffle]) % N_BATCH
    owners = owners.reshape(-1).astype(jnp.int32)
    one_hot = (owners[:, None] == jnp.arange(N_BATCH)[None, :]).astype(jnp.int32)
    page_rank = jnp.sum((jnp.cumsum(one_hot, axis=0) - one_hot) * one_hot, axis=1)
    places = shuffled_rows(key_places, N_BATCH, APD)
    position = places[owners, page_rank].astype(jnp.int32)
    lengths = jax.random.randint(key_lengths, (N_BATCH * NEW_DEV,), 1, P_SIZE * PAGE + 1)
    spot = jax.random.randint(key_spot, (), 0, N_BATCH * NEW_DEV)
    lengths = jnp.where(jnp.arange(N_BATCH * NEW_DEV) == spot, P_SIZE * PAGE, lengths).reshape(N_BATCH, NEW_DEV)
    request = position // P_SIZE
    within = position % P_SIZE
    tokens = jnp.clip(lengths[owners, request] - PAGE * within, 0, PAGE).astype(jnp.int32)
    return (owners, position, tokens)


def draw_queries(key, part):
    key = jax.random.fold_in(key, 11)
    shape = (REQUESTS, STEPS, HQ, HD)
    values = jax.random.normal(key, shape, jnp.float32) * 2.0
    values = jnp.clip(values, -8.0, 8.0)
    return values.reshape(REQUESTS, STEPS, HQ * HD).astype(jnp.bfloat16)


def draw_new_kv(key, part):
    key = jax.random.fold_in(key, 13)
    shape = (REQUESTS, STEPS, KV_COPIES, 2, HD)
    values = jax.random.normal(key, shape, jnp.float32)
    values = jnp.clip(values, -6.0, 6.0)
    return values.reshape(REQUESTS, STEPS, KV_COPIES * 2 * HD).astype(jnp.bfloat16)


def draw_block_table(key, part):
    key = jax.random.fold_in(key, 3)
    orders = shuffled_rows(key, N_BATCH, POOL)
    return orders.reshape(N_BATCH * OLD_DEV, P_SIZE).astype(jnp.int32)


def draw_old_lengths(key, part):
    key = jax.random.fold_in(key, 5)
    first, second = jax.random.split(key)
    lengths = jax.random.randint(first, (N_BATCH, OLD_DEV), 1, P_SIZE * PAGE + 1)
    spot = jax.random.randint(second, (N_BATCH,), 0, OLD_DEV)
    lengths = jnp.where(jnp.arange(OLD_DEV)[None, :] == spot[:, None], P_SIZE * PAGE, lengths)
    return lengths.reshape(-1).astype(jnp.int32)


def draw_new_slots(key, part):
    key = jax.random.fold_in(key, 7)
    orders = shuffled_rows(key, N_BATCH, REQ_DEV)
    chosen = jnp.sort(orders[:, :NEW_DEV], axis=1)
    return chosen.reshape(-1).astype(jnp.int32)


def draw_page_owner(key, part):
    owners, position, tokens = arrival_plan(key)
    return owners


def draw_page_position(key, part):
    owners, position, tokens = arrival_plan(key)
    return position


def draw_page_tokens(key, part):
    owners, position, tokens = arrival_plan(key)
    return tokens


def level_of(key, extent, cuts, smallest, high):
    def one(axis_at, blocks):
        heights = jax.random.uniform(jax.random.fold_in(jax.random.fold_in(key, 6), axis_at), (blocks,), jnp.float32, smallest / len(cuts), high / len(cuts))
        return jnp.repeat(jnp.exp(heights), extent[axis_at] // blocks).reshape((-1,) + (1,) * (len(extent) - axis_at - 1))

    level = one(*cuts[0])
    for cut in cuts[1:]:
        level = level * one(*cut)
    return level


def gaussian(stream_key, extent, width, reach, cuts=(), kind=jnp.bfloat16):
    factor_of = level_of(stream_key, extent, cuts, -0.22, 0.18) if cuts else 1.0
    array = jax.random.normal(stream_key, extent, jnp.float32) * width * factor_of
    return jnp.minimum(jnp.maximum(array, -reach), reach).astype(kind)


def setup_inputs(seed: int = 0) -> dict:
    seeds = jax.random.split(jax.random.key(seed), 11)
    return {
        "queries": draw_queries(jax.random.fold_in(seeds[10], 71), 0),
        "new_kv": draw_new_kv(jax.random.fold_in(seeds[10], 71), 0),
        "resident_pages": gaussian(seeds[2], (N_BATCH * POOL, PAGE, KV_COPIES * 2 * HD), 1.0, 6.0, ((0, 32), (2, 16))),
        "arriving_pages": gaussian(seeds[3], (N_BATCH * APD, PAGE, KV_HEADS * 2 * HD), 1.0, 6.0, ((0, 32), (1, 16))),
        "block_table": draw_block_table(jax.random.fold_in(seeds[10], 71), 0),
        "old_lengths": draw_old_lengths(jax.random.fold_in(seeds[10], 71), 0),
        "new_slots": draw_new_slots(jax.random.fold_in(seeds[10], 71), 0),
        "page_owner": draw_page_owner(jax.random.fold_in(seeds[10], 71), 0),
        "page_position": draw_page_position(jax.random.fold_in(seeds[10], 71), 0),
        "page_tokens": draw_page_tokens(jax.random.fold_in(seeds[10], 71), 0),
    }


masked_value = -1e+30

def widen_heads(page_data, repeats):
    shaped = page_data.reshape(page_data.shape[:-1] + (KV_HEADS, 2 * HD))
    shaped = jnp.repeat(shaped, repeats, axis=-2)
    return shaped.reshape(page_data.shape[:-1] + (KV_HEADS * repeats * 2 * HD,))

def attend(queries, fresh_rows, key_cache, key_valid):
    row_count = queries.shape[0]
    step_count = queries.shape[1]
    copies = key_cache.shape[2] // (2 * HD)
    per_copy = queries.shape[2] // (HD * copies)
    factor = 1.0 / math.sqrt(HD)
    query_view = queries.astype(jnp.float32).reshape(row_count, step_count, copies, per_copy, HD)
    cache_view = key_cache.astype(jnp.float32).reshape(row_count, key_cache.shape[1], copies, 2, HD)
    fresh_view = fresh_rows.astype(jnp.float32).reshape(row_count, step_count, copies, 2, HD)
    old_scores = jnp.einsum('rsvgd,rkvd->rsvgk', query_view, cache_view[:, :, :, 0]) * factor
    new_scores = jnp.einsum('rsvgd,rtvd->rsvgt', query_view, fresh_view[:, :, :, 0]) * factor
    causal = jnp.arange(step_count)[None, :] <= jnp.arange(step_count)[:, None]
    old_scores = jnp.where(key_valid[:, None, None, None, :], old_scores, masked_value)
    new_scores = jnp.where(causal[None, :, None, None, :], new_scores, masked_value)
    largest = jnp.maximum(lax.optimization_barrier(jnp.max(old_scores, axis=-1)), lax.optimization_barrier(jnp.max(new_scores, axis=-1)))
    old_weights = jnp.exp(old_scores - largest[..., None])
    new_weights = jnp.exp(new_scores - largest[..., None])
    denominator = lax.optimization_barrier(jnp.sum(old_weights, axis=-1)) + lax.optimization_barrier(jnp.sum(new_weights, axis=-1))
    old_rounded = lax.optimization_barrier(old_weights.astype(jnp.bfloat16)).astype(jnp.float32)
    new_rounded = lax.optimization_barrier(new_weights.astype(jnp.bfloat16)).astype(jnp.float32)
    weighted = jnp.einsum('rsvgk,rkvd->rsvgd', old_rounded, cache_view[:, :, :, 1])
    weighted = weighted + jnp.einsum('rsvgt,rtvd->rsvgd', new_rounded, fresh_view[:, :, :, 1])
    result = weighted / denominator[..., None]
    return result.astype(jnp.bfloat16).reshape(row_count, step_count, copies * per_copy * HD)

def reference(queries, new_kv, resident_pages, arriving_pages, block_table, old_lengths, new_slots, page_owner, page_position, page_tokens):
    repeats = KV_COPIES // KV_HEADS
    arrived_all = jnp.zeros((N_BATCH, APD) + arriving_pages.shape[1:], arriving_pages.dtype)
    arrived_all = arrived_all.at[page_owner, page_position].set(arriving_pages)
    tokens_all = jnp.zeros((N_BATCH, APD), jnp.int32).at[page_owner, page_position].set(page_tokens)

    def one_group(group_id):
        arrived = widen_heads(arrived_all[group_id], repeats)
        resident = lax.dynamic_slice_in_dim(resident_pages, group_id * POOL, POOL, 0)
        page_pool = jnp.concatenate([resident, arrived], axis=0)
        fresh_slots = lax.dynamic_slice_in_dim(new_slots, group_id * NEW_DEV, NEW_DEV, 0)
        new_flag = jnp.zeros((REQ_DEV,), jnp.int32).at[fresh_slots].set(1)
        old_slots = jnp.argsort(new_flag, stable=True)[:OLD_DEV].astype(jnp.int32)
        slot_order = jnp.concatenate([old_slots, fresh_slots.astype(jnp.int32)])
        new_table = (POOL + jnp.arange(NEW_DEV)[:, None] * P_SIZE + jnp.arange(P_SIZE)[None, :]).astype(jnp.int32)
        old_table = lax.dynamic_slice_in_dim(block_table, group_id * OLD_DEV, OLD_DEV, 0).astype(jnp.int32)
        page_table = jnp.concatenate([old_table, new_table], axis=0)
        key_cache = page_pool[page_table].reshape(REQ_DEV, P_SIZE * PAGE, page_pool.shape[2])
        lengths = lax.dynamic_slice_in_dim(old_lengths, group_id * OLD_DEV, OLD_DEV, 0)
        key_index = jnp.arange(P_SIZE * PAGE)
        old_valid = key_index[None, :] < lengths[:, None]
        counts = tokens_all[group_id].reshape(NEW_DEV, P_SIZE)
        new_valid = (jnp.arange(PAGE)[None, None, :] < counts[:, :, None]).reshape(NEW_DEV, P_SIZE * PAGE)
        key_valid = jnp.concatenate([old_valid, new_valid], axis=0)
        group_queries = lax.dynamic_slice_in_dim(queries, group_id * REQ_DEV, REQ_DEV, 0)[slot_order]
        group_fresh = lax.dynamic_slice_in_dim(new_kv, group_id * REQ_DEV, REQ_DEV, 0)[slot_order]
        result = attend(group_queries, group_fresh, key_cache, key_valid)
        placed = jnp.zeros_like(result).at[slot_order].set(result)
        return (placed, arrived)
    results, arrived = lax.map(one_group, jnp.arange(N_BATCH, dtype=jnp.int32))
    attention_out = results.reshape(REQUESTS, STEPS, HQ * HD)
    arrived_pages = arrived.reshape(N_BATCH * APD, PAGE, KV_COPIES * 2 * HD)
    return (attention_out, arrived_pages)
```

```python
import functools
import math

import jax
import jax.numpy as jnp
from jax import lax
from jax.experimental import pallas as pl
from jax.experimental.pallas import tpu as pltpu
from jax.sharding import PartitionSpec as P

HD = 128
KV_HEADS = 8
MASKED = -1e30
MESH = pl.DeviceIdType.MESH
ANY = pl.BlockSpec(memory_space=pl.ANY)
VMEM = pl.BlockSpec(memory_space=pltpu.VMEM)


def start(copies):
    for copy in copies:
        copy.start()


def wait(copies):
    for copy in copies:
        copy.wait()


def exchange_kernel(
    queries,
    new_kv,
    resident_pages,
    arriving_pages,
    block_table,
    old_lengths,
    new_slots,
    page_owner,
    page_position,
    page_tokens,
    attention_out,
    arrived,
    queries_v,
    new_kv_v,
    resident_v,
    arriving_v,
    table_s,
    lengths_s,
    slots_s,
    owner_s,
    position_s,
    tokens_s,
    send_table_v,
    send_table_s,
    pick_v,
    pick_s,
    key_send,
    key_recv,
    key_turn,
    key_rows,
    value_rows,
    value_send,
    value_recv,
    query_rows,
    fresh_rows,
    result_rows,
    results,
    load_sems,
    table_sems,
    send_sems,
    recv_sems,
):
    groups = lax.axis_size("batch")
    chips = lax.axis_size("tensor") // 2
    me = lax.axis_index("batch")
    place = lax.axis_index("tensor")
    chip = place // 2
    core = place % 2
    half = chip // (chips // 2)
    local = half == core
    pages = arriving_v.shape[0]
    old_count = table_s.shape[0]
    pages_each = table_s.shape[1]
    new_count = slots_s.shape[0]
    request_count = queries_v.shape[0]
    part = KV_HEADS * 4

    barrier = pltpu.get_barrier_semaphore()

    def greet_group(k, carry):
        other = lax.rem(me + k, groups)
        pl.semaphore_signal(barrier, inc=1, device_id=(other, place), device_id_type=MESH)
        return carry

    lax.fori_loop(1, groups, greet_group, 0)

    def greet_place(k, carry):
        other = core * chips + k

        @pl.when(other != place)
        def _():
            pl.semaphore_signal(barrier, inc=1, device_id=(me, other), device_id_type=MESH)

        return carry

    lax.fori_loop(0, chips, greet_place, 0)
    sibling = chip * 2 + 1 - core
    pl.semaphore_signal(barrier, inc=1, device_id=(me, sibling), device_id_type=MESH)

    loads = [
        pltpu.make_async_copy(page_owner, owner_s, load_sems.at[0]),
        pltpu.make_async_copy(arriving_pages, arriving_v, load_sems.at[1]),
        pltpu.make_async_copy(page_position, position_s, load_sems.at[2]),
        pltpu.make_async_copy(page_tokens, tokens_s, load_sems.at[3]),
        pltpu.make_async_copy(block_table, table_s, load_sems.at[4]),
        pltpu.make_async_copy(old_lengths, lengths_s, load_sems.at[5]),
        pltpu.make_async_copy(new_slots, slots_s, load_sems.at[6]),
        pltpu.make_async_copy(queries, queries_v, load_sems.at[7]),
        pltpu.make_async_copy(new_kv, new_kv_v, load_sems.at[8]),
        pltpu.make_async_copy(resident_pages, resident_v, load_sems.at[9]),
    ]
    start(loads)

    row = lax.broadcasted_iota(jnp.int32, (8, 128), 0)
    lane = lax.broadcasted_iota(jnp.int32, (8, 128), 1)
    loads[0].wait()
    first = jnp.zeros((8, 128), jnp.int32)
    last = jnp.zeros((8, 128), jnp.int32)
    for i in range(pages):
        j = pages - 1 - i
        last = jnp.where(lane == owner_s[me * pages + i], i, last)
        first = jnp.where(lane == owner_s[me * pages + j], j, first)
    send_table_v[...] = jnp.where(row == 0, first, last)
    copy = pltpu.make_async_copy(send_table_v, send_table_s, table_sems.at[0])
    copy.start()
    copy.wait()
    loads[1].wait()

    def pack_keys(g, carry):
        for r in range(2):
            page = arriving_v[send_table_s[r, g]]
            for h in range(KV_HEADS):
                key_send[g, r, h] = page[:, 2 * h * HD : (2 * h + 1) * HD]
        return carry

    lax.fori_loop(0, groups, pack_keys, 0)

    pl.semaphore_wait(barrier, groups - 1 + chips + jnp.where(local, 0, 1))

    def to_groups(source, target, n):
        own = pltpu.make_async_copy(source.at[me], target.at[me], recv_sems.at[n])
        own.start()

        def send(k, carry):
            other = lax.rem(me + k, groups)
            pltpu.make_async_remote_copy(
                src_ref=source.at[other],
                dst_ref=target.at[me],
                send_sem=send_sems.at[n],
                recv_sem=recv_sems.at[n],
                device_id=(other, place),
                device_id_type=MESH,
            ).start()
            return carry

        lax.fori_loop(1, groups, send, 0)

    def groups_arrived(target, n):
        pltpu.make_async_copy(target, target, recv_sems.at[n]).wait()

    def groups_sent(source, n):
        part_sent = source.at[pl.ds(0, groups - 1)]
        pltpu.make_async_copy(part_sent, part_sent, send_sems.at[n]).wait()

    def to_chips(source_of, target, n):
        slot = lax.rem(chip, chips // 2) * 2 + core

        @pl.when(local)
        def _():
            pltpu.make_async_copy(source_of(chip), target.at[slot], recv_sems.at[n]).start()

        @pl.when(jnp.logical_not(local))
        def _():
            pltpu.make_async_remote_copy(
                src_ref=source_of(chip),
                dst_ref=target.at[slot],
                send_sem=send_sems.at[n],
                recv_sem=recv_sems.at[n],
                device_id=(me, sibling),
                device_id_type=MESH,
            ).start()

        def send(k, carry):
            other = lax.rem(chip + k, chips)
            pltpu.make_async_remote_copy(
                src_ref=source_of(other),
                dst_ref=target.at[slot],
                send_sem=send_sems.at[n],
                recv_sem=recv_sems.at[n],
                device_id=(me, other * 2 + half),
                device_id_type=MESH,
            ).start()
            return carry

        lax.fori_loop(1, chips, send, 0)

    def chips_arrived(target, n):
        pltpu.make_async_copy(target, target, recv_sems.at[n]).wait()

    def chips_sent(target, n):
        most = target.at[pl.ds(0, chips - 1)]
        pltpu.make_async_copy(most, most, send_sems.at[n]).wait()

        @pl.when(jnp.logical_not(local))
        def _():
            pltpu.make_async_copy(target.at[0], target.at[0], send_sems.at[n]).wait()

    to_groups(key_send, key_recv, 0)
    to_chips(
        lambda h: arriving_v.at[:, :, pl.ds(pl.multiple_of((2 * h + 1) * HD, HD), HD)],
        value_rows,
        1,
    )

    loads[2].wait()
    loads[3].wait()

    def pick(b, carry):
        chosen, counts = carry
        seen = 0
        for i in range(pages):
            j = b * pages + i
            mine = owner_s[j] == me
            hit = lane == jnp.where(mine, position_s[j], -1)
            chosen = jnp.where(hit, 2 * b + seen, chosen)
            counts = jnp.where(hit, tokens_s[j], counts)
            seen = jnp.where(mine, 1, seen)
        return chosen, counts

    zero = jnp.zeros((8, 128), jnp.int32)
    chosen, counts = lax.fori_loop(0, groups, pick, (zero, zero))
    pick_v[...] = jnp.where(row == 0, chosen, counts)
    copy = pltpu.make_async_copy(pick_v, pick_s, table_sems.at[1])
    copy.start()
    copy.wait()
    wait(loads[4:])

    fresh_rows[...] = jnp.zeros_like(fresh_rows)
    factor = 1.0 / math.sqrt(HD)

    def attend(slot, index, cache, length):
        query = queries_v[slot].astype(jnp.float32)
        for g in range(part // 4):
            query_rows[4 * g : 4 * g + 4, :] = query[:, g * HD : (g + 1) * HD]
        fresh_rows[0:4, :] = new_kv_v[slot].astype(jnp.float32)
        fresh = fresh_rows[...].astype(jnp.bfloat16)
        keys = jnp.concatenate([k for k, _ in cache] + [fresh[:, :HD]], axis=0)
        values = jnp.concatenate([v for _, v in cache] + [fresh[:, HD:]], axis=0)
        cached = keys.shape[0] - fresh.shape[0]
        scores = lax.dot_general(
            query_rows[...].astype(jnp.bfloat16),
            keys,
            (((1,), (1,)), ((), ())),
            preferred_element_type=jnp.float32,
        )
        scores = scores * factor
        column = lax.broadcasted_iota(jnp.int32, scores.shape, 1)
        step = lax.rem(lax.broadcasted_iota(jnp.int32, scores.shape, 0), 4)
        bound = jnp.where(column < cached, length, cached + 1 + step)
        scores = jnp.where(column < bound, scores, MASKED)
        largest = jnp.max(scores, axis=1, keepdims=True)
        weights = jnp.exp(scores - largest)
        denominator = jnp.sum(weights, axis=1, keepdims=True)
        weighted = jnp.dot(
            weights.astype(jnp.bfloat16), values, preferred_element_type=jnp.float32
        )
        result_rows[...] = weighted / denominator
        for g in range(part // 4):
            results[index, :, g * HD : (g + 1) * HD] = result_rows[4 * g : 4 * g + 4, :]

    def resident(m, carry):
        slot = m
        for k in range(new_count):
            slot = slot + jnp.where(slots_s[k] <= slot, 1, 0)
        cache = []
        for j in range(pages_each):
            page = resident_v[table_s[m, j]]
            cache.append((page[:, :HD], page[:, HD:]))
        attend(slot, m, cache, lengths_s[m])
        return carry

    lax.fori_loop(0, 4, resident, 0)

    chips_arrived(value_rows, 1)

    def pack_values(g, carry):
        for r in range(2):
            page = value_rows[:, send_table_s[r, g]]
            value_send[g, r] = page.reshape(part, HD)
        return carry

    lax.fori_loop(0, groups, pack_values, 0)
    to_groups(value_send, value_recv, 2)

    lax.fori_loop(4, 6, resident, 0)

    groups_arrived(key_recv, 0)

    def turn_keys(p, carry):
        spot = pick_s[0, p]
        page = key_recv[spot // 2, spot % 2]
        for h in range(KV_HEADS):
            key_turn[h, p] = page[h]
        return carry

    lax.fori_loop(0, pages, turn_keys, 0)
    to_chips(lambda h: key_turn.at[h], key_rows, 3)

    lax.fori_loop(6, old_count, resident, 0)

    chips_arrived(key_rows, 3)
    mine = pl.ds(pl.multiple_of(core * part, part), part)

    def place_keys(p, carry):
        arrived[p, mine, :HD] = key_rows[:, p].reshape(part, HD)
        return carry

    lax.fori_loop(0, pages, place_keys, 0)

    def to_sibling(columns, n):
        return pltpu.make_async_remote_copy(
            src_ref=arrived.at[:, mine, columns],
            dst_ref=arrived.at[:, mine, columns],
            send_sem=send_sems.at[n],
            recv_sem=recv_sems.at[n],
            device_id=(me, sibling),
            device_id_type=MESH,
        )

    key_half = to_sibling(pl.ds(0, HD), 4)
    key_half.start()

    groups_arrived(value_recv, 2)

    def place_values(p, carry):
        spot = pick_s[0, p]
        arrived[p, mine, HD:] = value_recv[spot // 2, spot % 2]
        return carry

    lax.fori_loop(0, pages, place_values, 0)
    value_half = to_sibling(pl.ds(HD, HD), 5)
    value_half.start()
    key_half.wait()
    value_half.wait()

    def fresh_request(k, carry):
        length = 0
        cache = []
        for j in range(pages_each):
            length = length + pick_s[1, k * pages_each + j]
            page = arrived[k * pages_each + j]
            cache.append((page[:, :HD], page[:, HD:]))
        attend(slots_s[k], old_count + k, cache, length)
        return carry

    lax.fori_loop(0, new_count, fresh_request, 0)

    def put(r, carry):
        before = 0
        is_new = 0
        for k in range(new_count):
            before = before + jnp.where(slots_s[k] < r, 1, 0)
            is_new = is_new + jnp.where(slots_s[k] == r, 1, 0)
        index = jnp.where(is_new > 0, old_count + jnp.minimum(before, new_count - 1), jnp.maximum(r - before, 0))
        attention_out[r] = results[index].astype(jnp.bfloat16)
        return carry

    lax.fori_loop(0, request_count, put, 0)

    groups_sent(key_send, 0)
    chips_sent(value_rows, 1)
    groups_sent(value_send, 2)
    chips_sent(key_rows, 3)


def on_device(
    queries,
    new_kv,
    resident_pages,
    arriving_pages,
    block_table,
    old_lengths,
    new_slots,
    page_owner,
    page_position,
    page_tokens,
):
    groups = lax.axis_size("batch")
    pages = arriving_pages.shape[0]
    page_size = resident_pages.shape[1]
    bf16 = jnp.bfloat16
    dma = pltpu.SemaphoreType.DMA
    return pl.pallas_call(
        exchange_kernel,
        name="exchange_and_attend",
        out_shape=(
            jax.ShapeDtypeStruct(queries.shape, queries.dtype),
            jax.ShapeDtypeStruct((pages,) + resident_pages.shape[1:], bf16),
        ),
        in_specs=[ANY] * 10,
        out_specs=(VMEM, VMEM),
        scratch_shapes=[
            pltpu.VMEM(queries.shape, bf16),
            pltpu.VMEM(new_kv.shape, bf16),
            pltpu.VMEM(resident_pages.shape, bf16),
            pltpu.VMEM(arriving_pages.shape, bf16),
            pltpu.SMEM(block_table.shape, jnp.int32),
            pltpu.SMEM(old_lengths.shape, jnp.int32),
            pltpu.SMEM(new_slots.shape, jnp.int32),
            pltpu.SMEM(page_owner.shape, jnp.int32),
            pltpu.SMEM(page_position.shape, jnp.int32),
            pltpu.SMEM(page_tokens.shape, jnp.int32),
            pltpu.VMEM((8, 128), jnp.int32),
            pltpu.SMEM((8, 128), jnp.int32),
            pltpu.VMEM((8, 128), jnp.int32),
            pltpu.SMEM((8, 128), jnp.int32),
            pltpu.VMEM((groups, 2, KV_HEADS, 4, HD), bf16),
            pltpu.VMEM((groups, 2, KV_HEADS, 4, HD), bf16),
            pltpu.VMEM((KV_HEADS, pages, 4, HD), bf16),
            pltpu.VMEM((KV_HEADS, pages, 4, HD), bf16),
            pltpu.VMEM((KV_HEADS, pages, 4, HD), bf16),
            pltpu.VMEM((groups, 2, page_size // 2, HD), bf16),
            pltpu.VMEM((groups, 2, page_size // 2, HD), bf16),
            pltpu.VMEM((page_size // 2, HD), jnp.float32),
            pltpu.VMEM((16, 2 * HD), jnp.float32),
            pltpu.VMEM((page_size // 2, HD), jnp.float32),
            pltpu.VMEM(queries.shape, jnp.float32),
            dma((10,)),
            dma((2,)),
            dma((6,)),
            dma((6,)),
        ],
        compiler_params=pltpu.CompilerParams(
            collective_id=0, has_side_effects=True, vmem_limit_bytes=48 << 20
        ),
    )(
        queries,
        new_kv,
        resident_pages,
        arriving_pages,
        block_table,
        old_lengths,
        new_slots,
        page_owner,
        page_position,
        page_tokens,
    )


def solution(mesh):
    return jax.shard_map(
        on_device,
        mesh=mesh,
        in_specs=(
            P("batch", None, "tensor"),
            P("batch", None, "tensor"),
            P("batch", None, "tensor"),
            P("batch", "tensor", None),
            P("batch", None),
            P("batch"),
            P("batch"),
            P(),
            P(),
            P(),
        ),
        out_specs=(P("batch", None, "tensor"), P("batch", None, "tensor")),
        check_vma=False,
    )
```

```python
import functools
import math

import jax
import jax.numpy as jnp
from jax import lax
from jax.experimental import pallas as pl
from jax.experimental.pallas import tpu as pltpu
from jax.sharding import PartitionSpec as P

HD = 128
KV_HEADS = 8
MASKED = -1e30
MESH = pl.DeviceIdType.MESH
ANY = pl.BlockSpec(memory_space=pl.ANY)
VMEM = pl.BlockSpec(memory_space=pltpu.VMEM)


def start(copies):
    for copy in copies:
        copy.start()


def wait(copies):
    for copy in copies:
        copy.wait()


def exchange_kernel(
    queries,
    new_kv,
    resident_pages,
    arriving_pages,
    block_table,
    old_lengths,
    new_slots,
    page_owner,
    page_position,
    page_tokens,
    attention_out,
    arrived,
    queries_v,
    new_kv_v,
    resident_v,
    arriving_v,
    table_s,
    lengths_s,
    slots_s,
    owner_s,
    position_s,
    tokens_s,
    send_table_v,
    send_table_s,
    pick_v,
    pick_s,
    key_send,
    key_recv,
    key_turn,
    key_rows,
    value_rows,
    value_send,
    value_recv,
    query_rows,
    fresh_rows,
    result_rows,
    results,
    load_sems,
    table_sems,
    send_sems,
    recv_sems,
):
    groups = lax.axis_size("batch")
    chips = lax.axis_size("tensor") // 2
    me = lax.axis_index("batch")
    place = lax.axis_index("tensor")
    chip = place // 2
    core = place % 2
    half = chip // (chips // 2)
    local = half == core
    pages = arriving_v.shape[0]
    old_count = table_s.shape[1]
    pages_each = table_s.shape[0]
    new_count = slots_s.shape[0]
    request_count = queries_v.shape[0]
    part = KV_HEADS * 4

    barrier = pltpu.get_barrier_semaphore()

    def greet_group(k, carry):
        other = lax.rem(me + k, groups)
        pl.semaphore_signal(barrier, inc=1, device_id=(other, place), device_id_type=MESH)
        return carry

    lax.fori_loop(1, groups, greet_group, 0)

    def greet_place(k, carry):
        other = core * chips + k

        @pl.when(other != place)
        def _():
            pl.semaphore_signal(barrier, inc=1, device_id=(me, other), device_id_type=MESH)

        return carry

    lax.fori_loop(0, chips, greet_place, 0)
    sibling = chip * 2 + 1 - core
    pl.semaphore_signal(barrier, inc=1, device_id=(me, sibling), device_id_type=MESH)

    loads = [
        pltpu.make_async_copy(page_owner, owner_s, load_sems.at[0]),
        pltpu.make_async_copy(arriving_pages, arriving_v, load_sems.at[1]),
        pltpu.make_async_copy(page_position, position_s, load_sems.at[2]),
        pltpu.make_async_copy(page_tokens, tokens_s, load_sems.at[3]),
        pltpu.make_async_copy(block_table, table_s, load_sems.at[4]),
        pltpu.make_async_copy(old_lengths, lengths_s, load_sems.at[5]),
        pltpu.make_async_copy(new_slots, slots_s, load_sems.at[6]),
        pltpu.make_async_copy(queries, queries_v, load_sems.at[7]),
        pltpu.make_async_copy(new_kv, new_kv_v, load_sems.at[8]),
        pltpu.make_async_copy(resident_pages, resident_v, load_sems.at[9]),
    ]
    start(loads)

    row = lax.broadcasted_iota(jnp.int32, (8, 128), 0)
    lane = lax.broadcasted_iota(jnp.int32, (8, 128), 1)
    loads[0].wait()
    first = jnp.zeros((8, 128), jnp.int32)
    last = jnp.zeros((8, 128), jnp.int32)
    for i in range(pages):
        j = pages - 1 - i
        last = jnp.where(lane == owner_s[me * pages + i], i, last)
        first = jnp.where(lane == owner_s[me * pages + j], j, first)
    send_table_v[...] = jnp.where(row == 0, first, last)
    copy = pltpu.make_async_copy(send_table_v, send_table_s, table_sems.at[0])
    copy.start()
    copy.wait()
    loads[1].wait()

    def pack_keys(g, carry):
        for r in range(2):
            page = arriving_v[send_table_s[r, g]]
            for h in range(KV_HEADS):
                key_send[g, r, h] = page[:, 2 * h * HD : (2 * h + 1) * HD]
        return carry

    lax.fori_loop(0, groups, pack_keys, 0)

    pl.semaphore_wait(barrier, groups - 1 + chips + jnp.where(local, 0, 1))

    def to_groups(source, target, n):
        own = pltpu.make_async_copy(source.at[me], target.at[me], recv_sems.at[n])
        own.start()

        def send(k, carry):
            other = lax.rem(me + k, groups)
            pltpu.make_async_remote_copy(
                src_ref=source.at[other],
                dst_ref=target.at[me],
                send_sem=send_sems.at[n],
                recv_sem=recv_sems.at[n],
                device_id=(other, place),
                device_id_type=MESH,
            ).start()
            return carry

        lax.fori_loop(1, groups, send, 0)

    def groups_arrived(target, n):
        pltpu.make_async_copy(target, target, recv_sems.at[n]).wait()

    def groups_sent(source, n):
        part_sent = source.at[pl.ds(0, groups - 1)]
        pltpu.make_async_copy(part_sent, part_sent, send_sems.at[n]).wait()

    def to_chips(source_of, target, n):
        slot = lax.rem(chip, chips // 2) * 2 + core

        @pl.when(local)
        def _():
            pltpu.make_async_copy(source_of(chip), target.at[slot], recv_sems.at[n]).start()

        @pl.when(jnp.logical_not(local))
        def _():
            pltpu.make_async_remote_copy(
                src_ref=source_of(chip),
                dst_ref=target.at[slot],
                send_sem=send_sems.at[n],
                recv_sem=recv_sems.at[n],
                device_id=(me, sibling),
                device_id_type=MESH,
            ).start()

        def send(k, carry):
            other = lax.rem(chip + k, chips)
            pltpu.make_async_remote_copy(
                src_ref=source_of(other),
                dst_ref=target.at[slot],
                send_sem=send_sems.at[n],
                recv_sem=recv_sems.at[n],
                device_id=(me, other * 2 + half),
                device_id_type=MESH,
            ).start()
            return carry

        lax.fori_loop(1, chips, send, 0)

    def chips_arrived(target, n):
        pltpu.make_async_copy(target, target, recv_sems.at[n]).wait()

    def chips_sent(target, n):
        most = target.at[pl.ds(0, chips - 1)]
        pltpu.make_async_copy(most, most, send_sems.at[n]).wait()

        @pl.when(jnp.logical_not(local))
        def _():
            pltpu.make_async_copy(target.at[0], target.at[0], send_sems.at[n]).wait()

    to_groups(key_send, key_recv, 0)
    to_chips(
        lambda h: arriving_v.at[:, :, pl.ds(pl.multiple_of((2 * h + 1) * HD, HD), HD)],
        value_rows,
        1,
    )

    loads[2].wait()
    loads[3].wait()

    def pick(b, carry):
        chosen, counts = carry
        seen = 0
        for i in range(pages):
            j = b * pages + i
            mine = owner_s[j] == me
            hit = lane == jnp.where(mine, position_s[j], -1)
            chosen = jnp.where(hit, 2 * b + seen, chosen)
            counts = jnp.where(hit, tokens_s[j], counts)
            seen = jnp.where(mine, 1, seen)
        return chosen, counts

    zero = jnp.zeros((8, 128), jnp.int32)
    chosen, counts = lax.fori_loop(0, groups, pick, (zero, zero))
    pick_v[...] = jnp.where(row == 0, chosen, counts)
    copy = pltpu.make_async_copy(pick_v, pick_s, table_sems.at[1])
    copy.start()
    copy.wait()
    wait(loads[4:])

    fresh_rows[...] = jnp.zeros_like(fresh_rows)
    factor = 1.0 / math.sqrt(HD)

    def attend(slot, index, cache, length):
        query = queries_v[slot].astype(jnp.float32)
        for g in range(part // 4):
            query_rows[4 * g : 4 * g + 4, :] = query[:, g * HD : (g + 1) * HD]
        fresh_rows[0:4, :] = new_kv_v[slot].astype(jnp.float32)
        fresh = fresh_rows[...].astype(jnp.bfloat16)
        keys = jnp.concatenate([k for k, _ in cache] + [fresh[:, :HD]], axis=0)
        values = jnp.concatenate([v for _, v in cache] + [fresh[:, HD:]], axis=0)
        cached = keys.shape[0] - fresh.shape[0]
        scores = lax.dot_general(
            query_rows[...].astype(jnp.bfloat16),
            keys,
            (((1,), (1,)), ((), ())),
            preferred_element_type=jnp.float32,
        )
        scores = scores * factor
        column = lax.broadcasted_iota(jnp.int32, scores.shape, 1)
        step = lax.rem(lax.broadcasted_iota(jnp.int32, scores.shape, 0), 4)
        bound = jnp.where(column < cached, length, cached + 1 + step)
        scores = jnp.where(column < bound, scores, MASKED)
        largest = jnp.max(scores, axis=1, keepdims=True)
        weights = jnp.exp(scores - largest)
        denominator = jnp.sum(weights, axis=1, keepdims=True)
        weighted = jnp.dot(
            weights.astype(jnp.bfloat16), values, preferred_element_type=jnp.float32
        )
        result_rows[...] = weighted / denominator
        for g in range(part // 4):
            results[index, :, g * HD : (g + 1) * HD] = result_rows[4 * g : 4 * g + 4, :]

    def resident(m, carry):
        slot = m
        for k in range(new_count):
            slot = slot + jnp.where(slots_s[k] <= slot, 1, 0)
        cache = []
        for j in range(pages_each):
            page = resident_v[table_s[j, m]]
            cache.append((page[:, :HD], page[:, HD:]))
        attend(slot, m, cache, lengths_s[m])
        return carry

    lax.fori_loop(0, 4, resident, 0)

    chips_arrived(value_rows, 1)

    def pack_values(g, carry):
        for r in range(2):
            page = value_rows[:, send_table_s[r, g]]
            value_send[g, r] = page.reshape(part, HD)
        return carry

    lax.fori_loop(0, groups, pack_values, 0)
    to_groups(value_send, value_recv, 2)

    lax.fori_loop(4, 6, resident, 0)

    groups_arrived(key_recv, 0)

    def turn_keys(p, carry):
        spot = pick_s[0, p]
        page = key_recv[spot // 2, spot % 2]
        for h in range(KV_HEADS):
            key_turn[h, p] = page[h]
        return carry

    lax.fori_loop(0, pages, turn_keys, 0)
    to_chips(lambda h: key_turn.at[h], key_rows, 3)

    lax.fori_loop(6, old_count, resident, 0)

    chips_arrived(key_rows, 3)
    mine = pl.ds(pl.multiple_of(core * part, part), part)

    def place_keys(p, carry):
        arrived[p, mine, :HD] = key_rows[:, p].reshape(part, HD)
        return carry

    lax.fori_loop(0, pages, place_keys, 0)

    def to_sibling(columns, n):
        return pltpu.make_async_remote_copy(
            src_ref=arrived.at[:, mine, columns],
            dst_ref=arrived.at[:, mine, columns],
            send_sem=send_sems.at[n],
            recv_sem=recv_sems.at[n],
            device_id=(me, sibling),
            device_id_type=MESH,
        )

    key_half = to_sibling(pl.ds(0, HD), 4)
    key_half.start()

    groups_arrived(value_recv, 2)

    def place_values(p, carry):
        spot = pick_s[0, p]
        arrived[p, mine, HD:] = value_recv[spot // 2, spot % 2]
        return carry

    lax.fori_loop(0, pages, place_values, 0)
    value_half = to_sibling(pl.ds(HD, HD), 5)
    value_half.start()
    key_half.wait()
    value_half.wait()

    def fresh_request(k, carry):
        length = 0
        cache = []
        for j in range(pages_each):
            length = length + pick_s[1, k * pages_each + j]
            page = arrived[k * pages_each + j]
            cache.append((page[:, :HD], page[:, HD:]))
        attend(slots_s[k], old_count + k, cache, length)
        return carry

    lax.fori_loop(0, new_count, fresh_request, 0)

    def put(r, carry):
        before = 0
        is_new = 0
        for k in range(new_count):
            before = before + jnp.where(slots_s[k] < r, 1, 0)
            is_new = is_new + jnp.where(slots_s[k] == r, 1, 0)
        index = jnp.where(is_new > 0, old_count + jnp.minimum(before, new_count - 1), jnp.maximum(r - before, 0))
        attention_out[r] = results[index].astype(jnp.bfloat16)
        return carry

    lax.fori_loop(0, request_count, put, 0)

    groups_sent(key_send, 0)
    chips_sent(value_rows, 1)
    groups_sent(value_send, 2)
    chips_sent(key_rows, 3)


def on_device(
    queries,
    new_kv,
    resident_pages,
    arriving_pages,
    block_table,
    old_lengths,
    new_slots,
    page_owner,
    page_position,
    page_tokens,
):
    groups = lax.axis_size("batch")
    pages = arriving_pages.shape[0]
    page_size = resident_pages.shape[1]
    bf16 = jnp.bfloat16
    dma = pltpu.SemaphoreType.DMA
    return pl.pallas_call(
        exchange_kernel,
        name="exchange_and_attend",
        out_shape=(
            jax.ShapeDtypeStruct(queries.shape, queries.dtype),
            jax.ShapeDtypeStruct((pages,) + resident_pages.shape[1:], bf16),
        ),
        in_specs=[ANY] * 10,
        out_specs=(VMEM, VMEM),
        scratch_shapes=[
            pltpu.VMEM(queries.shape, bf16),
            pltpu.VMEM(new_kv.shape, bf16),
            pltpu.VMEM(resident_pages.shape, bf16),
            pltpu.VMEM(arriving_pages.shape, bf16),
            pltpu.SMEM(block_table.shape[::-1], jnp.int32),
            pltpu.SMEM(old_lengths.shape, jnp.int32),
            pltpu.SMEM(new_slots.shape, jnp.int32),
            pltpu.SMEM(page_owner.shape, jnp.int32),
            pltpu.SMEM(page_position.shape, jnp.int32),
            pltpu.SMEM(page_tokens.shape, jnp.int32),
            pltpu.VMEM((8, 128), jnp.int32),
            pltpu.SMEM((8, 128), jnp.int32),
            pltpu.VMEM((8, 128), jnp.int32),
            pltpu.SMEM((8, 128), jnp.int32),
            pltpu.VMEM((groups, 2, KV_HEADS, 4, HD), bf16),
            pltpu.VMEM((groups, 2, KV_HEADS, 4, HD), bf16),
            pltpu.VMEM((KV_HEADS, pages, 4, HD), bf16),
            pltpu.VMEM((KV_HEADS, pages, 4, HD), bf16),
            pltpu.VMEM((KV_HEADS, pages, 4, HD), bf16),
            pltpu.VMEM((groups, 2, page_size // 2, HD), bf16),
            pltpu.VMEM((groups, 2, page_size // 2, HD), bf16),
            pltpu.VMEM((page_size // 2, HD), jnp.float32),
            pltpu.VMEM((16, 2 * HD), jnp.float32),
            pltpu.VMEM((page_size // 2, HD), jnp.float32),
            pltpu.VMEM(queries.shape, jnp.float32),
            dma((10,)),
            dma((2,)),
            dma((6,)),
            dma((6,)),
        ],
        compiler_params=pltpu.CompilerParams(
            collective_id=0, has_side_effects=True, vmem_limit_bytes=48 << 20
        ),
    )(
        *(
            pltpu.with_memory_space_constraint(x, pltpu.HBM)
            for x in (
                queries,
                new_kv,
                resident_pages,
                arriving_pages,
                block_table.T,
                old_lengths,
                new_slots,
                page_owner,
                page_position,
                page_tokens,
            )
        )
    )


def solution(mesh):
    return jax.shard_map(
        on_device,
        mesh=mesh,
        in_specs=(
            P("batch", None, "tensor"),
            P("batch", None, "tensor"),
            P("batch", None, "tensor"),
            P("batch", "tensor", None),
            P("batch", None),
            P("batch"),
            P("batch"),
            P(),
            P(),
            P(),
        ),
        out_specs=(P("batch", None, "tensor"), P("batch", None, "tensor")),
        check_vma=False,
    )
```

```python
import functools
import math

import jax
import jax.numpy as jnp
from jax import lax
from jax.experimental import pallas as pl
from jax.experimental.pallas import tpu as pltpu
from jax.sharding import PartitionSpec as P

HD = 128
KV_HEADS = 8
MASKED = -1e30
MESH = pl.DeviceIdType.MESH
ANY = pl.BlockSpec(memory_space=pl.ANY)
VMEM = pl.BlockSpec(memory_space=pltpu.VMEM)


def start(copies):
    for copy in copies:
        copy.start()


def wait(copies):
    for copy in copies:
        copy.wait()


def split_rows(rows, staging, target, index):
    staging[...] = rows
    for g in range(rows.shape[0] // 4):
        piece = staging[4 * g : 4 * g + 4, :].astype(jnp.bfloat16)
        target[index, :, g * HD : (g + 1) * HD] = piece


def finish_kernel(
    arrived,
    results,
    fresh_weights,
    fresh_sums,
    denominators,
    new_slots,
    attention_out,
    arrived_out,
    slots_s,
    rows_v,
    sems,
):
    slots_copy = pltpu.make_async_copy(new_slots, slots_s, sems.at[0])
    slots_copy.start()
    copy = pltpu.make_async_copy(arrived, arrived_out, sems.at[1])
    copy.start()
    other = 1 - lax.axis_index("tensor") % 2
    part = rows_v.shape[0]
    others = pl.ds(pl.multiple_of(other * part, part), part)
    new_count = fresh_sums.shape[0]
    pages_each = arrived.shape[0] // new_count
    slots_copy.wait()
    for m in range(results.shape[0]):
        slot = m
        for k in range(new_count):
            slot = slot + jnp.where(slots_s[k] <= slot, 1, 0)
        attention_out[slot] = results[m]
    for k in range(new_count):
        first_page = k * pages_each
        values = jnp.concatenate(
            [arrived[first_page + j, others, HD:] for j in range(pages_each)], axis=0
        )
        rows = jnp.dot(fresh_weights[k, other], values, preferred_element_type=jnp.float32)
        rows = (fresh_sums[k] + rows) / denominators[k]
        split_rows(rows, rows_v, attention_out, slots_s[k])
    copy.wait()


def exchange_kernel(
    queries,
    new_kv,
    resident_pages,
    arriving_pages,
    block_table,
    old_lengths,
    new_slots,
    page_owner,
    page_position,
    page_tokens,
    arrived,
    results,
    fresh_weights,
    fresh_sums,
    denominators,
    queries_v,
    new_kv_v,
    resident_v,
    arriving_v,
    table_s,
    lengths_s,
    slots_s,
    owner_s,
    position_s,
    tokens_s,
    send_table_v,
    send_table_s,
    pick_v,
    pick_s,
    key_send,
    key_recv,
    key_turn,
    key_rows,
    value_rows,
    value_send,
    value_recv,
    query_rows,
    fresh_rows,
    result_rows,
    load_sems,
    table_sems,
    send_sems,
    recv_sems,
):
    groups = lax.axis_size("batch")
    chips = lax.axis_size("tensor") // 2
    me = lax.axis_index("batch")
    place = lax.axis_index("tensor")
    chip = place // 2
    core = place % 2
    half = chip // (chips // 2)
    local = half == core
    pages = arriving_v.shape[0]
    old_count = table_s.shape[1]
    pages_each = table_s.shape[0]
    new_count = slots_s.shape[0]
    page_size = arrived.shape[1]
    part = KV_HEADS * 4

    loads = [
        pltpu.make_async_copy(page_owner, owner_s, load_sems.at[0]),
        pltpu.make_async_copy(arriving_pages, arriving_v, load_sems.at[1]),
        pltpu.make_async_copy(page_position, position_s, load_sems.at[2]),
        pltpu.make_async_copy(page_tokens, tokens_s, load_sems.at[3]),
        pltpu.make_async_copy(block_table, table_s, load_sems.at[4]),
        pltpu.make_async_copy(old_lengths, lengths_s, load_sems.at[5]),
        pltpu.make_async_copy(new_slots, slots_s, load_sems.at[6]),
        pltpu.make_async_copy(queries, queries_v, load_sems.at[7]),
        pltpu.make_async_copy(new_kv, new_kv_v, load_sems.at[8]),
        pltpu.make_async_copy(resident_pages, resident_v, load_sems.at[9]),
    ]
    start(loads[:2])

    barrier = pltpu.get_barrier_semaphore()

    def peer(k):
        return jnp.where(k < me, k, k + 1)

    def greet_group(k, carry):
        pl.semaphore_signal(barrier, inc=1, device_id=(peer(k), place), device_id_type=MESH)
        return carry

    lax.fori_loop(0, groups - 1, greet_group, 0)

    def greet_place(k, carry):
        other = core * chips + k

        @pl.when(other != place)
        def _():
            pl.semaphore_signal(barrier, inc=1, device_id=(me, other), device_id_type=MESH)

        return carry

    lax.fori_loop(0, chips, greet_place, 0)
    sibling = chip * 2 + 1 - core
    pl.semaphore_signal(barrier, inc=1, device_id=(me, sibling), device_id_type=MESH)
    start(loads[2:])

    row = lax.broadcasted_iota(jnp.int32, (8, 128), 0)
    lane = lax.broadcasted_iota(jnp.int32, (8, 128), 1)
    loads[0].wait()
    first = jnp.zeros((8, 128), jnp.int32)
    last = jnp.zeros((8, 128), jnp.int32)
    for i in range(pages):
        j = pages - 1 - i
        last = jnp.where(lane == owner_s[me * pages + i], i, last)
        first = jnp.where(lane == owner_s[me * pages + j], j, first)
    send_table_v[...] = jnp.where(row == 0, first, last)
    copy = pltpu.make_async_copy(send_table_v, send_table_s, table_sems.at[0])
    copy.start()
    copy.wait()
    loads[1].wait()

    def pack_keys(g, carry):
        for r in range(2):
            page = send_table_s[r, g]
            for h in range(KV_HEADS):
                key_send[g, r, h] = arriving_v[page, :, 2 * h * HD : (2 * h + 1) * HD]
        return carry

    lax.fori_loop(0, groups, pack_keys, 0, unroll=4)

    pl.semaphore_wait(barrier, groups - 1 + chips + jnp.where(local, 0, 1))

    def to_groups(source, target, n):
        own = pltpu.make_async_copy(source.at[me], target.at[me], recv_sems.at[n])
        own.start()

        def send(k, carry):
            other = peer(k)
            pltpu.make_async_remote_copy(
                src_ref=source.at[other],
                dst_ref=target.at[me],
                send_sem=send_sems.at[n],
                recv_sem=recv_sems.at[n],
                device_id=(other, place),
                device_id_type=MESH,
            ).start()
            return carry

        lax.fori_loop(0, groups - 1, send, 0)

    def groups_arrived(target, n):
        pltpu.make_async_copy(target, target, recv_sems.at[n]).wait()

    def groups_sent(source, n):
        part_sent = source.at[pl.ds(0, groups - 1)]
        pltpu.make_async_copy(part_sent, part_sent, send_sems.at[n]).wait()

    def to_chips(source_of, target, n):
        slot = lax.rem(chip, chips // 2) * 2 + core

        @pl.when(local)
        def _():
            pltpu.make_async_copy(source_of(chip), target.at[slot], recv_sems.at[n]).start()

        @pl.when(jnp.logical_not(local))
        def _():
            pltpu.make_async_remote_copy(
                src_ref=source_of(chip),
                dst_ref=target.at[slot],
                send_sem=send_sems.at[n],
                recv_sem=recv_sems.at[n],
                device_id=(me, sibling),
                device_id_type=MESH,
            ).start()

        def send(k, carry):
            other = lax.rem(chip + k, chips)
            pltpu.make_async_remote_copy(
                src_ref=source_of(other),
                dst_ref=target.at[slot],
                send_sem=send_sems.at[n],
                recv_sem=recv_sems.at[n],
                device_id=(me, other * 2 + half),
                device_id_type=MESH,
            ).start()
            return carry

        lax.fori_loop(1, chips, send, 0)

    def chips_arrived(target, n):
        pltpu.make_async_copy(target, target, recv_sems.at[n]).wait()

    def chips_sent(target, n):
        most = target.at[pl.ds(0, chips - 1)]
        pltpu.make_async_copy(most, most, send_sems.at[n]).wait()

        @pl.when(jnp.logical_not(local))
        def _():
            pltpu.make_async_copy(target.at[0], target.at[0], send_sems.at[n]).wait()

    to_groups(key_send, key_recv, 0)
    to_chips(
        lambda h: arriving_v.at[:, :, pl.ds(pl.multiple_of((2 * h + 1) * HD, HD), HD)],
        value_rows,
        1,
    )

    wait(loads[4:])

    fresh_rows[...] = jnp.zeros_like(fresh_rows)
    factor = 1.0 / math.sqrt(HD)

    def read_query(slot):
        query = queries_v[slot].astype(jnp.float32)
        for g in range(part // 4):
            query_rows[4 * g : 4 * g + 4, :] = query[:, g * HD : (g + 1) * HD]
        fresh_rows[0:4, :] = new_kv_v[slot].astype(jnp.float32)
        return query_rows[...].astype(jnp.bfloat16), fresh_rows[...].astype(jnp.bfloat16)

    def score(query, keys):
        return factor * lax.dot_general(
            query, keys, (((1,), (1,)), ((), ())), preferred_element_type=jnp.float32
        )

    def weigh(weights, values):
        return jnp.dot(weights.astype(jnp.bfloat16), values, preferred_element_type=jnp.float32)

    def store_result(index, rows):
        split_rows(rows, result_rows, results, index)

    def columns_of(scores):
        return lax.broadcasted_iota(jnp.int32, scores.shape, 1)

    def rows_of(scores):
        return lax.broadcasted_iota(jnp.int32, scores.shape, 0)

    def resident(m, carry):
        slot = m
        for k in range(new_count):
            slot = slot + jnp.where(slots_s[k] <= slot, 1, 0)
        query, fresh = read_query(slot)
        pages_read = [resident_v[table_s[j, m]] for j in range(pages_each)]
        cache = jnp.concatenate(pages_read + [fresh], axis=0)
        scores = score(query, cache[:, :HD])
        column = columns_of(scores)
        step = lax.rem(rows_of(scores), 4)
        cached = pages_each * page_size
        bound = jnp.where(column < cached, lengths_s[m], cached + 1 + step)
        scores = jnp.where(column < bound, scores, MASKED)
        largest = jnp.max(scores, axis=1, keepdims=True)
        weights = jnp.exp(scores - largest)
        denominator = jnp.sum(weights, axis=1, keepdims=True)
        store_result(m, weigh(weights, cache[:, HD:]) / denominator)
        return carry

    lax.fori_loop(0, 3, resident, 0)

    chips_arrived(value_rows, 1)

    def pack_values(g, carry):
        for r in range(2):
            page = value_rows[:, send_table_s[r, g]]
            value_send[g, r] = page.reshape(part, HD)
        return carry

    lax.fori_loop(0, groups, pack_values, 0, unroll=2)
    to_groups(value_send, value_recv, 2)

    loads[2].wait()
    loads[3].wait()

    def pick(b, carry):
        chosen, counts = carry
        seen = 0
        for i in range(pages):
            j = b * pages + i
            mine = owner_s[j] == me
            hit = lane == jnp.where(mine, position_s[j], -1)
            chosen = jnp.where(hit, 2 * b + seen, chosen)
            counts = jnp.where(hit, tokens_s[j], counts)
            seen = jnp.where(mine, 1, seen)
        return chosen, counts

    zero = jnp.zeros((8, 128), jnp.int32)
    chosen, counts = lax.fori_loop(0, groups, pick, (zero, zero))
    pick_v[...] = jnp.where(row == 0, chosen, counts)
    copy = pltpu.make_async_copy(pick_v, pick_s, table_sems.at[1])
    copy.start()
    copy.wait()
    lax.fori_loop(3, 7, resident, 0)

    groups_arrived(key_recv, 0)

    def turn_keys(p, carry):
        spot = pick_s[0, p]
        page = key_recv[spot // 2, spot % 2]
        for h in range(KV_HEADS):
            key_turn[h, p] = page[h]
        return carry

    lax.fori_loop(0, pages, turn_keys, 0, unroll=4)
    to_chips(lambda h: key_turn.at[h], key_rows, 3)

    lax.fori_loop(7, old_count, resident, 0)

    chips_arrived(key_rows, 3)
    mine = pl.ds(pl.multiple_of(core * part, part), part)

    def place_keys(p, carry):
        arrived[p, mine, :HD] = key_rows[:, p].reshape(part, HD)
        return carry

    lax.fori_loop(0, pages, place_keys, 0, unroll=4)

    def to_sibling(columns, n):
        return pltpu.make_async_remote_copy(
            src_ref=arrived.at[:, mine, columns],
            dst_ref=arrived.at[:, mine, columns],
            send_sem=send_sems.at[n],
            recv_sem=recv_sems.at[n],
            device_id=(me, sibling),
            device_id_type=MESH,
        )

    key_half = to_sibling(pl.ds(0, HD), 4)
    key_half.start()

    key_half.wait()

    def half_of(k, rows, columns):
        first_page = k * pages_each
        return jnp.concatenate(
            [arrived[first_page + j, rows, columns] for j in range(pages_each)], axis=0
        )

    def fresh_scores(k, carry):
        length = 0
        for j in range(pages_each):
            length = length + pick_s[1, k * pages_each + j]
        query, fresh = read_query(slots_s[k])
        scores = []
        for c in range(2):
            keys = half_of(k, pl.ds(c * part, part), pl.ds(0, HD))
            cached = score(query, keys)
            column = columns_of(cached)
            position = column // part * page_size + c * part + column % part
            scores.append(jnp.where(position < length, cached, MASKED))
        own = score(query, fresh[:, :HD])
        scores.append(jnp.where(columns_of(own) <= lax.rem(rows_of(own), 4), own, MASKED))
        largest = functools.reduce(
            jnp.maximum, [jnp.max(x, axis=1, keepdims=True) for x in scores]
        )
        weights = [jnp.exp(x - largest) for x in scores]
        denominator = sum(jnp.sum(x, axis=1, keepdims=True) for x in weights)
        for c in range(2):
            fresh_weights[k, c] = weights[c].astype(jnp.bfloat16)
        fresh_sums[k] = weigh(weights[2], fresh[:, HD:])
        denominators[k] = jnp.broadcast_to(denominator, denominators.shape[1:])
        return carry

    lax.fori_loop(0, new_count, fresh_scores, 0)

    groups_arrived(value_recv, 2)

    def place_values(p, carry):
        spot = pick_s[0, p]
        arrived[p, mine, HD:] = value_recv[spot // 2, spot % 2]
        return carry

    lax.fori_loop(0, pages, place_values, 0, unroll=7)
    value_half = to_sibling(pl.ds(HD, HD), 5)
    value_half.start()

    for k in range(new_count):
        fresh_sums[k] += weigh(fresh_weights[k, core], half_of(k, mine, pl.ds(HD, HD)))

    value_half.wait()

    groups_sent(key_send, 0)
    chips_sent(value_rows, 1)
    groups_sent(value_send, 2)
    chips_sent(key_rows, 3)


def on_device(
    queries,
    new_kv,
    resident_pages,
    arriving_pages,
    block_table,
    old_lengths,
    new_slots,
    page_owner,
    page_position,
    page_tokens,
):
    groups = lax.axis_size("batch")
    pages = arriving_pages.shape[0]
    page_size = resident_pages.shape[1]
    new_count = new_slots.shape[0]
    bf16 = jnp.bfloat16
    dma = pltpu.SemaphoreType.DMA
    half_keys = pages // new_count * page_size // 2
    rows = (new_count, page_size // 2, HD)
    partial = pl.pallas_call(
        exchange_kernel,
        name="exchange_and_attend",
        out_shape=(
            jax.ShapeDtypeStruct((pages,) + resident_pages.shape[1:], bf16),
            jax.ShapeDtypeStruct(block_table.shape[:1] + queries.shape[1:], bf16),
            jax.ShapeDtypeStruct((new_count, 2, page_size // 2, half_keys), bf16),
            jax.ShapeDtypeStruct(rows, jnp.float32),
            jax.ShapeDtypeStruct(rows, jnp.float32),
        ),
        in_specs=[ANY] * 10,
        out_specs=(VMEM,) * 5,
        scratch_shapes=[
            pltpu.VMEM(queries.shape, bf16),
            pltpu.VMEM(new_kv.shape, bf16),
            pltpu.VMEM(resident_pages.shape, bf16),
            pltpu.VMEM(arriving_pages.shape, bf16),
            pltpu.SMEM(block_table.shape[::-1], jnp.int32),
            pltpu.SMEM(old_lengths.shape, jnp.int32),
            pltpu.SMEM(new_slots.shape, jnp.int32),
            pltpu.SMEM(page_owner.shape, jnp.int32),
            pltpu.SMEM(page_position.shape, jnp.int32),
            pltpu.SMEM(page_tokens.shape, jnp.int32),
            pltpu.VMEM((8, 128), jnp.int32),
            pltpu.SMEM((8, 128), jnp.int32),
            pltpu.VMEM((8, 128), jnp.int32),
            pltpu.SMEM((8, 128), jnp.int32),
            pltpu.VMEM((groups, 2, KV_HEADS, 4, HD), bf16),
            pltpu.VMEM((groups, 2, KV_HEADS, 4, HD), bf16),
            pltpu.VMEM((KV_HEADS, pages, 4, HD), bf16),
            pltpu.VMEM((KV_HEADS, pages, 4, HD), bf16),
            pltpu.VMEM((KV_HEADS, pages, 4, HD), bf16),
            pltpu.VMEM((groups, 2, page_size // 2, HD), bf16),
            pltpu.VMEM((groups, 2, page_size // 2, HD), bf16),
            pltpu.VMEM((page_size // 2, HD), jnp.float32),
            pltpu.VMEM((16, 2 * HD), jnp.float32),
            pltpu.VMEM((page_size // 2, HD), jnp.float32),
            dma((10,)),
            dma((2,)),
            dma((6,)),
            dma((6,)),
        ],
        compiler_params=pltpu.CompilerParams(
            collective_id=0, has_side_effects=True, vmem_limit_bytes=48 << 20
        ),
    )(
        *(
            pltpu.with_memory_space_constraint(x, pltpu.HBM)
            for x in (
                queries,
                new_kv,
                resident_pages,
                arriving_pages,
                block_table.T,
                old_lengths,
                new_slots,
                page_owner,
                page_position,
                page_tokens,
            )
        )
    )

    return pl.pallas_call(
        finish_kernel,
        name="finish_fresh",
        out_shape=(
            jax.ShapeDtypeStruct(queries.shape, bf16),
            jax.ShapeDtypeStruct((pages,) + resident_pages.shape[1:], bf16),
        ),
        in_specs=[VMEM] * 5 + [ANY],
        out_specs=(VMEM, ANY),
        scratch_shapes=[
            pltpu.SMEM(new_slots.shape, jnp.int32),
            pltpu.VMEM((page_size // 2, HD), jnp.float32),
            dma((2,)),
        ],
        compiler_params=pltpu.CompilerParams(vmem_limit_bytes=16 << 20),
    )(*partial, pltpu.with_memory_space_constraint(new_slots, pltpu.HBM))


def solution(mesh):
    return jax.shard_map(
        on_device,
        mesh=mesh,
        in_specs=(
            P("batch", None, "tensor"),
            P("batch", None, "tensor"),
            P("batch", None, "tensor"),
            P("batch", "tensor", None),
            P("batch", None),
            P("batch"),
            P("batch"),
            P(),
            P(),
            P(),
        ),
        out_specs=(P("batch", None, "tensor"), P("batch", None, "tensor")),
        check_vma=False,
    )
```

```python
import functools
import math

import jax
import jax.numpy as jnp
from jax import lax
from jax.experimental import pallas as pl
from jax.experimental.pallas import tpu as pltpu
from jax.sharding import PartitionSpec as P

HD = 128
KV_HEADS = 8
MASKED = -1e30
MESH = pl.DeviceIdType.MESH
ANY = pl.BlockSpec(memory_space=pl.ANY)
VMEM = pl.BlockSpec(memory_space=pltpu.VMEM)


def start(copies):
    for copy in copies:
        copy.start()


def wait(copies):
    for copy in copies:
        copy.wait()


def split_rows(rows, staging, target, index):
    staging[...] = rows
    for g in range(rows.shape[0] // 4):
        piece = staging[4 * g : 4 * g + 4, :].astype(jnp.bfloat16)
        target[index, :, g * HD : (g + 1) * HD] = piece


def finish_kernel(
    arrived,
    results,
    fresh_weights,
    fresh_sums,
    denominators,
    new_slots,
    attention_out,
    arrived_out,
    slots_s,
    rows_v,
    attention_v,
    sems,
):
    slots_copy = pltpu.make_async_copy(new_slots, slots_s, sems.at[0])
    slots_copy.start()
    copy = pltpu.make_async_copy(arrived, arrived_out, sems.at[1])
    copy.start()
    other = 1 - lax.axis_index("tensor") % 2
    part = rows_v.shape[0]
    others = pl.ds(pl.multiple_of(other * part, part), part)
    new_count = fresh_sums.shape[0]
    pages_each = arrived.shape[0] // new_count
    fresh = []
    for k in range(new_count):
        first_page = k * pages_each
        values = jnp.concatenate(
            [arrived[first_page + j, others, HD:] for j in range(pages_each)], axis=0
        )
        rows = jnp.dot(fresh_weights[k, other], values, preferred_element_type=jnp.float32)
        fresh.append((fresh_sums[k] + rows) / denominators[k])
    slots_copy.wait()
    for m in range(results.shape[0]):
        slot = m
        for k in range(new_count):
            slot = slot + jnp.where(slots_s[k] <= slot, 1, 0)
        attention_v[slot] = results[m]
    for k in range(new_count):
        split_rows(fresh[k], rows_v, attention_v, slots_s[k])
    out = pltpu.make_async_copy(attention_v, attention_out, sems.at[2])
    out.start()
    copy.wait()
    out.wait()


def exchange_kernel(
    queries,
    new_kv,
    resident_pages,
    arriving_pages,
    block_table,
    old_lengths,
    new_slots,
    page_owner,
    page_position,
    page_tokens,
    arrived,
    results,
    fresh_weights,
    fresh_sums,
    denominators,
    queries_v,
    new_kv_v,
    resident_v,
    arriving_v,
    table_s,
    lengths_s,
    slots_s,
    owner_s,
    position_s,
    tokens_s,
    send_table_v,
    send_table_s,
    pick_v,
    pick_s,
    key_send,
    key_recv,
    key_turn,
    key_rows,
    value_rows,
    value_send,
    value_recv,
    query_rows,
    fresh_rows,
    result_rows,
    load_sems,
    table_sems,
    send_sems,
    recv_sems,
):
    groups = lax.axis_size("batch")
    chips = lax.axis_size("tensor") // 2
    me = lax.axis_index("batch")
    place = lax.axis_index("tensor")
    chip = place // 2
    core = place % 2
    half = chip // (chips // 2)
    local = half == core
    pages = arriving_v.shape[0]
    old_count = table_s.shape[1]
    pages_each = table_s.shape[0]
    new_count = slots_s.shape[0]
    page_size = arrived.shape[1]
    part = KV_HEADS * 4

    loads = [
        pltpu.make_async_copy(page_owner, owner_s, load_sems.at[0]),
        pltpu.make_async_copy(arriving_pages, arriving_v, load_sems.at[1]),
        pltpu.make_async_copy(page_position, position_s, load_sems.at[2]),
        pltpu.make_async_copy(page_tokens, tokens_s, load_sems.at[3]),
        pltpu.make_async_copy(block_table, table_s, load_sems.at[4]),
        pltpu.make_async_copy(old_lengths, lengths_s, load_sems.at[5]),
        pltpu.make_async_copy(new_slots, slots_s, load_sems.at[6]),
        pltpu.make_async_copy(queries, queries_v, load_sems.at[7]),
        pltpu.make_async_copy(new_kv, new_kv_v, load_sems.at[8]),
        pltpu.make_async_copy(resident_pages, resident_v, load_sems.at[9]),
    ]
    start(loads[:2])

    barrier = pltpu.get_barrier_semaphore()

    x0 = me // 8
    z0 = me % 8
    mine_at = jnp.where(x0 < 2, me, 16 + z0 % 4 * 4 + z0 // 4 * 2 + x0 % 2)

    def peer(k):
        at = jnp.where(k < mine_at, k, k + 1)
        i = at % 16
        return jnp.where(at < 16, at, (2 + i % 2) * 8 + i // 4 + i // 2 % 2 * 4)

    for dz in (4, 3, 5, 2, 6, 1, 7, 0):
        for dx in (2, 1, 3, 0):
            if dx or dz:
                other = (me // 8 + dx) % 4 * 8 + (me + dz) % 8
                pl.semaphore_signal(
                    barrier, inc=1, device_id=(other, place), device_id_type=MESH
                )

    def greet_place(k, carry):
        other = core * chips + k

        @pl.when(other != place)
        def _():
            pl.semaphore_signal(barrier, inc=1, device_id=(me, other), device_id_type=MESH)

        return carry

    lax.fori_loop(0, chips, greet_place, 0, unroll=True)
    sibling = chip * 2 + 1 - core
    pl.semaphore_signal(barrier, inc=1, device_id=(me, sibling), device_id_type=MESH)
    start(loads[2:])

    row = lax.broadcasted_iota(jnp.int32, (8, 128), 0)
    lane = lax.broadcasted_iota(jnp.int32, (8, 128), 1)
    loads[0].wait()
    first = jnp.zeros((8, 128), jnp.int32)
    last = jnp.zeros((8, 128), jnp.int32)
    for i in range(pages):
        j = pages - 1 - i
        last = jnp.where(lane == owner_s[me * pages + i], i, last)
        first = jnp.where(lane == owner_s[me * pages + j], j, first)
    send_table_v[...] = jnp.where(row == 0, first, last)
    copy = pltpu.make_async_copy(send_table_v, send_table_s, table_sems.at[0])
    copy.start()
    copy.wait()
    loads[1].wait()

    def pack_keys(g, carry):
        for r in range(2):
            page = send_table_s[r, g]
            for h in range(KV_HEADS):
                key_send[g, r, h] = arriving_v[page, :, 2 * h * HD : (2 * h + 1) * HD]
        return carry

    lax.fori_loop(0, groups, pack_keys, 0, unroll=4)

    pl.semaphore_wait(barrier, groups - 1 + chips + jnp.where(local, 0, 1))

    def to_groups(source, target, n):
        own = pltpu.make_async_copy(source.at[me], target.at[me], recv_sems.at[n])
        own.start()

        def send(k, carry):
            other = peer(k)
            pltpu.make_async_remote_copy(
                src_ref=source.at[other],
                dst_ref=target.at[me],
                send_sem=send_sems.at[n],
                recv_sem=recv_sems.at[n],
                device_id=(other, place),
                device_id_type=MESH,
            ).start()
            return carry

        lax.fori_loop(0, groups - 1, send, 0)

    def groups_arrived(target, n):
        pltpu.make_async_copy(target, target, recv_sems.at[n]).wait()

    def groups_sent(source, n):
        part_sent = source.at[pl.ds(0, groups - 1)]
        pltpu.make_async_copy(part_sent, part_sent, send_sems.at[n]).wait()

    def to_chips(source_of, target, n):
        slot = lax.rem(chip, chips // 2) * 2 + core

        @pl.when(local)
        def _():
            pltpu.make_async_copy(source_of(chip), target.at[slot], recv_sems.at[n]).start()

        @pl.when(jnp.logical_not(local))
        def _():
            pltpu.make_async_remote_copy(
                src_ref=source_of(chip),
                dst_ref=target.at[slot],
                send_sem=send_sems.at[n],
                recv_sem=recv_sems.at[n],
                device_id=(me, sibling),
                device_id_type=MESH,
            ).start()

        def send(k, carry):
            other = lax.rem(chip + k, chips)
            pltpu.make_async_remote_copy(
                src_ref=source_of(other),
                dst_ref=target.at[slot],
                send_sem=send_sems.at[n],
                recv_sem=recv_sems.at[n],
                device_id=(me, other * 2 + half),
                device_id_type=MESH,
            ).start()
            return carry

        lax.fori_loop(1, chips, send, 0)

    def chips_arrived(target, n):
        pltpu.make_async_copy(target, target, recv_sems.at[n]).wait()

    def chips_sent(target, n):
        most = target.at[pl.ds(0, chips - 1)]
        pltpu.make_async_copy(most, most, send_sems.at[n]).wait()

        @pl.when(jnp.logical_not(local))
        def _():
            pltpu.make_async_copy(target.at[0], target.at[0], send_sems.at[n]).wait()

    to_chips(
        lambda h: arriving_v.at[:, :, pl.ds(pl.multiple_of((2 * h + 1) * HD, HD), HD)],
        value_rows,
        1,
    )
    to_groups(key_send, key_recv, 0)

    wait(loads[2:])

    def pick(b, carry):
        chosen, counts = carry
        seen = 0
        for i in range(pages):
            j = b * pages + i
            mine = owner_s[j] == me
            hit = lane == jnp.where(mine, position_s[j], -1)
            chosen = jnp.where(hit, 2 * b + seen, chosen)
            counts = jnp.where(hit, tokens_s[j], counts)
            seen = jnp.where(mine, 1, seen)
        return chosen, counts

    zero = jnp.zeros((8, 128), jnp.int32)
    chosen, counts = lax.fori_loop(0, groups, pick, (zero, zero))
    pick_v[...] = jnp.where(row == 0, chosen, counts)
    copy = pltpu.make_async_copy(pick_v, pick_s, table_sems.at[1])
    copy.start()
    copy.wait()
    fresh_rows[...] = jnp.zeros_like(fresh_rows)
    factor = 1.0 / math.sqrt(HD)

    def read_query(slot):
        query = queries_v[slot].astype(jnp.float32)
        for g in range(part // 4):
            query_rows[4 * g : 4 * g + 4, :] = query[:, g * HD : (g + 1) * HD]
        fresh_rows[0:4, :] = new_kv_v[slot].astype(jnp.float32)
        return query_rows[...].astype(jnp.bfloat16), fresh_rows[...].astype(jnp.bfloat16)

    def score(query, keys):
        return factor * lax.dot_general(
            query, keys, (((1,), (1,)), ((), ())), preferred_element_type=jnp.float32
        )

    def weigh(weights, values):
        return jnp.dot(weights.astype(jnp.bfloat16), values, preferred_element_type=jnp.float32)

    def store_result(index, rows):
        split_rows(rows, result_rows, results, index)

    def columns_of(scores):
        return lax.broadcasted_iota(jnp.int32, scores.shape, 1)

    def rows_of(scores):
        return lax.broadcasted_iota(jnp.int32, scores.shape, 0)

    def resident(m, carry):
        slot = m
        for k in range(new_count):
            slot = slot + jnp.where(slots_s[k] <= slot, 1, 0)
        query, fresh = read_query(slot)
        pages_read = [resident_v[table_s[j, m]] for j in range(pages_each)]
        cache = jnp.concatenate(pages_read + [fresh], axis=0)
        scores = score(query, cache[:, :HD])
        column = columns_of(scores)
        step = lax.rem(rows_of(scores), 4)
        cached = pages_each * page_size
        bound = jnp.where(column < cached, lengths_s[m], cached + 1 + step)
        scores = jnp.where(column < bound, scores, MASKED)
        largest = jnp.max(scores, axis=1, keepdims=True)
        weights = jnp.exp(scores - largest)
        denominator = jnp.sum(weights, axis=1, keepdims=True)
        store_result(m, weigh(weights, cache[:, HD:]) / denominator)
        return carry

    lax.fori_loop(0, 5, resident, 0)

    chips_arrived(value_rows, 1)

    def pack_values(g, carry):
        for r in range(2):
            page = value_rows[:, send_table_s[r, g]]
            value_send[g, r] = page.reshape(part, HD)
        return carry

    lax.fori_loop(0, groups, pack_values, 0, unroll=2)
    to_groups(value_send, value_recv, 2)

    lax.fori_loop(5, 6, resident, 0)

    groups_arrived(key_recv, 0)

    def turn_keys(p, carry):
        spot = pick_s[0, p]
        page = key_recv[spot // 2, spot % 2]
        for h in range(KV_HEADS):
            key_turn[h, p] = page[h]
        return carry

    lax.fori_loop(0, pages, turn_keys, 0, unroll=4)
    to_chips(lambda h: key_turn.at[h], key_rows, 3)

    lax.fori_loop(6, old_count, resident, 0)

    chips_arrived(key_rows, 3)
    mine = pl.ds(pl.multiple_of(core * part, part), part)

    def place_keys(p, carry):
        arrived[p, mine, :HD] = key_rows[:, p].reshape(part, HD)
        return carry

    lax.fori_loop(0, pages, place_keys, 0, unroll=4)

    def to_sibling(columns, n):
        return pltpu.make_async_remote_copy(
            src_ref=arrived.at[:, mine, columns],
            dst_ref=arrived.at[:, mine, columns],
            send_sem=send_sems.at[n],
            recv_sem=recv_sems.at[n],
            device_id=(me, sibling),
            device_id_type=MESH,
        )

    key_half = to_sibling(pl.ds(0, HD), 4)
    key_half.start()

    key_half.wait()

    def half_of(k, rows, columns):
        first_page = k * pages_each
        return jnp.concatenate(
            [arrived[first_page + j, rows, columns] for j in range(pages_each)], axis=0
        )

    def fresh_scores(k, carry):
        length = 0
        for j in range(pages_each):
            length = length + pick_s[1, k * pages_each + j]
        query, fresh = read_query(slots_s[k])
        scores = []
        for c in range(2):
            keys = half_of(k, pl.ds(c * part, part), pl.ds(0, HD))
            cached = score(query, keys)
            column = columns_of(cached)
            position = column // part * page_size + c * part + column % part
            scores.append(jnp.where(position < length, cached, MASKED))
        own = score(query, fresh[:, :HD])
        scores.append(jnp.where(columns_of(own) <= lax.rem(rows_of(own), 4), own, MASKED))
        largest = functools.reduce(
            jnp.maximum, [jnp.max(x, axis=1, keepdims=True) for x in scores]
        )
        weights = [jnp.exp(x - largest) for x in scores]
        denominator = sum(jnp.sum(x, axis=1, keepdims=True) for x in weights)
        for c in range(2):
            fresh_weights[k, c] = weights[c].astype(jnp.bfloat16)
        fresh_sums[k] = weigh(weights[2], fresh[:, HD:])
        denominators[k] = jnp.broadcast_to(denominator, denominators.shape[1:])
        return carry

    lax.fori_loop(0, new_count, fresh_scores, 0)

    groups_arrived(value_recv, 2)

    def place_values(p, carry):
        spot = pick_s[0, p]
        arrived[p, mine, HD:] = value_recv[spot // 2, spot % 2]
        return carry

    lax.fori_loop(0, pages, place_values, 0, unroll=7)
    value_half = to_sibling(pl.ds(HD, HD), 5)
    value_half.start()

    for k in range(new_count):
        fresh_sums[k] += weigh(fresh_weights[k, core], half_of(k, mine, pl.ds(HD, HD)))

    value_half.wait()

    groups_sent(key_send, 0)
    chips_sent(value_rows, 1)
    groups_sent(value_send, 2)
    chips_sent(key_rows, 3)


def on_device(
    queries,
    new_kv,
    resident_pages,
    arriving_pages,
    block_table,
    old_lengths,
    new_slots,
    page_owner,
    page_position,
    page_tokens,
):
    groups = lax.axis_size("batch")
    pages = arriving_pages.shape[0]
    page_size = resident_pages.shape[1]
    new_count = new_slots.shape[0]
    bf16 = jnp.bfloat16
    dma = pltpu.SemaphoreType.DMA
    half_keys = pages // new_count * page_size // 2
    rows = (new_count, page_size // 2, HD)
    partial = pl.pallas_call(
        exchange_kernel,
        name="exchange_and_attend",
        out_shape=(
            jax.ShapeDtypeStruct((pages,) + resident_pages.shape[1:], bf16),
            jax.ShapeDtypeStruct(block_table.shape[:1] + queries.shape[1:], bf16),
            jax.ShapeDtypeStruct((new_count, 2, page_size // 2, half_keys), bf16),
            jax.ShapeDtypeStruct(rows, jnp.float32),
            jax.ShapeDtypeStruct(rows, jnp.float32),
        ),
        in_specs=[ANY] * 10,
        out_specs=(VMEM,) * 5,
        scratch_shapes=[
            pltpu.VMEM(queries.shape, bf16),
            pltpu.VMEM(new_kv.shape, bf16),
            pltpu.VMEM(resident_pages.shape, bf16),
            pltpu.VMEM(arriving_pages.shape, bf16),
            pltpu.SMEM(block_table.shape[::-1], jnp.int32),
            pltpu.SMEM(old_lengths.shape, jnp.int32),
            pltpu.SMEM(new_slots.shape, jnp.int32),
            pltpu.SMEM(page_owner.shape, jnp.int32),
            pltpu.SMEM(page_position.shape, jnp.int32),
            pltpu.SMEM(page_tokens.shape, jnp.int32),
            pltpu.VMEM((8, 128), jnp.int32),
            pltpu.SMEM((8, 128), jnp.int32),
            pltpu.VMEM((8, 128), jnp.int32),
            pltpu.SMEM((8, 128), jnp.int32),
            pltpu.VMEM((groups, 2, KV_HEADS, 4, HD), bf16),
            pltpu.VMEM((groups, 2, KV_HEADS, 4, HD), bf16),
            pltpu.VMEM((KV_HEADS, pages, 4, HD), bf16),
            pltpu.VMEM((KV_HEADS, pages, 4, HD), bf16),
            pltpu.VMEM((KV_HEADS, pages, 4, HD), bf16),
            pltpu.VMEM((groups, 2, page_size // 2, HD), bf16),
            pltpu.VMEM((groups, 2, page_size // 2, HD), bf16),
            pltpu.VMEM((page_size // 2, HD), jnp.float32),
            pltpu.VMEM((16, 2 * HD), jnp.float32),
            pltpu.VMEM((page_size // 2, HD), jnp.float32),
            dma((10,)),
            dma((2,)),
            dma((6,)),
            dma((6,)),
        ],
        compiler_params=pltpu.CompilerParams(
            collective_id=0, has_side_effects=True, vmem_limit_bytes=48 << 20
        ),
    )(
        *(
            pltpu.with_memory_space_constraint(x, pltpu.HBM)
            for x in (
                queries,
                new_kv,
                resident_pages,
                arriving_pages,
                block_table.T,
                old_lengths,
                new_slots,
                page_owner,
                page_position,
                page_tokens,
            )
        )
    )

    return pl.pallas_call(
        finish_kernel,
        name="finish_fresh",
        out_shape=(
            jax.ShapeDtypeStruct(queries.shape, bf16),
            jax.ShapeDtypeStruct((pages,) + resident_pages.shape[1:], bf16),
        ),
        in_specs=[VMEM] * 5 + [ANY],
        out_specs=(ANY, ANY),
        scratch_shapes=[
            pltpu.SMEM(new_slots.shape, jnp.int32),
            pltpu.VMEM((page_size // 2, HD), jnp.float32),
            pltpu.VMEM(queries.shape, bf16),
            dma((3,)),
        ],
        compiler_params=pltpu.CompilerParams(vmem_limit_bytes=16 << 20),
    )(*partial, pltpu.with_memory_space_constraint(new_slots, pltpu.HBM))


def solution(mesh):
    return jax.shard_map(
        on_device,
        mesh=mesh,
        in_specs=(
            P("batch", None, "tensor"),
            P("batch", None, "tensor"),
            P("batch", None, "tensor"),
            P("batch", "tensor", None),
            P("batch", None),
            P("batch"),
            P("batch"),
            P(),
            P(),
            P(),
        ),
        out_specs=(P("batch", None, "tensor"), P("batch", None, "tensor")),
        check_vma=False,
    )
```

```python
import functools
import math

import jax
import jax.numpy as jnp
from jax import lax
from jax.experimental import pallas as pl
from jax.experimental.pallas import tpu as pltpu
from jax.sharding import PartitionSpec as P

HD = 128
KV_HEADS = 8
MASKED = -1e30
MESH = pl.DeviceIdType.MESH
ANY = pl.BlockSpec(memory_space=pl.ANY)
VMEM = pl.BlockSpec(memory_space=pltpu.VMEM)

GROUP_ORDER = [*range(16)] + [x * 8 + z for z in (0, 1, 4, 2, 5, 3, 6, 7) for x in (2, 3)]


def start(copies):
    for copy in copies:
        copy.start()


def wait(copies):
    for copy in copies:
        copy.wait()


def split_rows(rows, staging, target, index):
    staging[...] = rows
    for g in range(rows.shape[0] // 4):
        piece = staging[4 * g : 4 * g + 4, :].astype(jnp.bfloat16)
        target[index, :, g * HD : (g + 1) * HD] = piece


def finish_kernel(
    arrived,
    results,
    fresh_weights,
    fresh_sums,
    denominators,
    new_slots,
    attention_out,
    arrived_out,
    slots_s,
    rows_v,
    fresh_v,
    attention_v,
    sems,
):
    slots_copy = pltpu.make_async_copy(new_slots, slots_s, sems.at[0])
    slots_copy.start()
    copy = pltpu.make_async_copy(arrived, arrived_out, sems.at[1])
    copy.start()
    other = 1 - lax.axis_index("tensor") % 2
    part = rows_v.shape[0]
    others = pl.ds(pl.multiple_of(other * part, part), part)
    new_count = fresh_sums.shape[0]
    pages_each = arrived.shape[0] // new_count
    for k in range(new_count):
        first_page = k * pages_each
        values = jnp.concatenate(
            [arrived[first_page + j, others, HD:] for j in range(pages_each)], axis=0
        )
        rows = jnp.dot(fresh_weights[k, other], values, preferred_element_type=jnp.float32)
        split_rows((fresh_sums[k] + rows) / denominators[k], rows_v, fresh_v, k)
    slots_copy.wait()
    for m in range(results.shape[0]):
        slot = m
        for k in range(new_count):
            slot = slot + jnp.where(slots_s[k] <= slot, 1, 0)
        attention_v[slot] = results[m]
    for k in range(new_count):
        attention_v[slots_s[k]] = fresh_v[k]
    out = pltpu.make_async_copy(attention_v, attention_out, sems.at[2])
    out.start()
    copy.wait()
    out.wait()


def exchange_kernel(
    queries,
    new_kv,
    resident_pages,
    arriving_pages,
    block_table,
    old_lengths,
    new_slots,
    page_owner,
    page_position,
    page_tokens,
    arrived,
    results,
    fresh_weights,
    fresh_sums,
    denominators,
    queries_v,
    new_kv_v,
    resident_v,
    arriving_v,
    table_s,
    lengths_s,
    slots_s,
    owner_s,
    position_s,
    tokens_s,
    send_table_v,
    send_table_s,
    pick_v,
    pick_s,
    key_send,
    key_recv,
    key_turn,
    key_rows,
    value_rows,
    value_send,
    value_recv,
    query_rows,
    fresh_rows,
    result_rows,
    load_sems,
    table_sems,
    send_sems,
    recv_sems,
):
    groups = lax.axis_size("batch")
    chips = lax.axis_size("tensor") // 2
    me = lax.axis_index("batch")
    place = lax.axis_index("tensor")
    chip = place // 2
    core = place % 2
    half = chip // (chips // 2)
    local = half == core
    pages = arriving_v.shape[0]
    old_count = table_s.shape[1]
    pages_each = table_s.shape[0]
    new_count = slots_s.shape[0]
    page_size = arrived.shape[1]
    part = KV_HEADS * 4

    loads = [
        pltpu.make_async_copy(page_owner, owner_s, load_sems.at[0]),
        pltpu.make_async_copy(arriving_pages, arriving_v, load_sems.at[1]),
        pltpu.make_async_copy(page_position, position_s, load_sems.at[2]),
        pltpu.make_async_copy(page_tokens, tokens_s, load_sems.at[3]),
        pltpu.make_async_copy(block_table, table_s, load_sems.at[4]),
        pltpu.make_async_copy(old_lengths, lengths_s, load_sems.at[5]),
        pltpu.make_async_copy(new_slots, slots_s, load_sems.at[6]),
        pltpu.make_async_copy(queries, queries_v, load_sems.at[7]),
        pltpu.make_async_copy(new_kv, new_kv_v, load_sems.at[8]),
        pltpu.make_async_copy(resident_pages, resident_v, load_sems.at[9]),
    ]
    start(loads[:2])

    barrier = pltpu.get_barrier_semaphore()

    for dz in (4, 3, 5, 2, 6, 1, 7, 0):
        for dx in (2, 1, 3, 0):
            if dx or dz:
                other = (me // 8 + dx) % 4 * 8 + (me + dz) % 8
                pl.semaphore_signal(
                    barrier, inc=1, device_id=(other, place), device_id_type=MESH
                )

    def greet_place(k, carry):
        other = core * chips + k

        @pl.when(other != place)
        def _():
            pl.semaphore_signal(barrier, inc=1, device_id=(me, other), device_id_type=MESH)

        return carry

    lax.fori_loop(0, chips, greet_place, 0, unroll=True)
    sibling = chip * 2 + 1 - core
    pl.semaphore_signal(barrier, inc=1, device_id=(me, sibling), device_id_type=MESH)
    start(loads[2:])

    row = lax.broadcasted_iota(jnp.int32, (8, 128), 0)
    lane = lax.broadcasted_iota(jnp.int32, (8, 128), 1)
    loads[0].wait()
    first = jnp.zeros((8, 128), jnp.int32)
    last = jnp.zeros((8, 128), jnp.int32)
    for i in range(pages):
        j = pages - 1 - i
        last = jnp.where(lane == owner_s[me * pages + i], i, last)
        first = jnp.where(lane == owner_s[me * pages + j], j, first)
    send_table_v[...] = jnp.where(row == 0, first, last)
    copy = pltpu.make_async_copy(send_table_v, send_table_s, table_sems.at[0])
    copy.start()
    copy.wait()
    loads[1].wait()

    def pack_keys(g, carry):
        for r in range(2):
            page = send_table_s[r, g]
            for h in range(KV_HEADS):
                key_send[g, r, h] = arriving_v[page, :, 2 * h * HD : (2 * h + 1) * HD]
        return carry

    lax.fori_loop(0, groups, pack_keys, 0, unroll=4)

    pl.semaphore_wait(barrier, groups - 1 + chips + jnp.where(local, 0, 1))

    def to_groups(source, target, n):
        own = pltpu.make_async_copy(source.at[me], target.at[me], recv_sems.at[n])
        own.start()

        for other in GROUP_ORDER:

            @pl.when(me != other)
            def _():
                pltpu.make_async_remote_copy(
                    src_ref=source.at[other],
                    dst_ref=target.at[me],
                    send_sem=send_sems.at[n],
                    recv_sem=recv_sems.at[n],
                    device_id=(other, place),
                    device_id_type=MESH,
                ).start()

    def groups_arrived(target, n):
        pltpu.make_async_copy(target, target, recv_sems.at[n]).wait()

    def groups_sent(source, n):
        part_sent = source.at[pl.ds(0, groups - 1)]
        pltpu.make_async_copy(part_sent, part_sent, send_sems.at[n]).wait()

    def to_chips(source_of, target, n):
        slot = lax.rem(chip, chips // 2) * 2 + core

        @pl.when(local)
        def _():
            pltpu.make_async_copy(source_of(chip), target.at[slot], recv_sems.at[n]).start()

        @pl.when(jnp.logical_not(local))
        def _():
            pltpu.make_async_remote_copy(
                src_ref=source_of(chip),
                dst_ref=target.at[slot],
                send_sem=send_sems.at[n],
                recv_sem=recv_sems.at[n],
                device_id=(me, sibling),
                device_id_type=MESH,
            ).start()

        def send(k, carry):
            other = lax.rem(chip + k, chips)
            pltpu.make_async_remote_copy(
                src_ref=source_of(other),
                dst_ref=target.at[slot],
                send_sem=send_sems.at[n],
                recv_sem=recv_sems.at[n],
                device_id=(me, other * 2 + half),
                device_id_type=MESH,
            ).start()
            return carry

        lax.fori_loop(1, chips, send, 0)

    def chips_arrived(target, n):
        pltpu.make_async_copy(target, target, recv_sems.at[n]).wait()

    def chips_sent(target, n):
        most = target.at[pl.ds(0, chips - 1)]
        pltpu.make_async_copy(most, most, send_sems.at[n]).wait()

        @pl.when(jnp.logical_not(local))
        def _():
            pltpu.make_async_copy(target.at[0], target.at[0], send_sems.at[n]).wait()

    to_chips(
        lambda h: arriving_v.at[:, :, pl.ds(pl.multiple_of((2 * h + 1) * HD, HD), HD)],
        value_rows,
        1,
    )
    to_groups(key_send, key_recv, 0)

    wait(loads[2:])

    def pick(b, carry):
        chosen, counts = carry
        seen = 0
        for i in range(pages):
            j = b * pages + i
            mine = owner_s[j] == me
            hit = lane == jnp.where(mine, position_s[j], -1)
            chosen = jnp.where(hit, 2 * b + seen, chosen)
            counts = jnp.where(hit, tokens_s[j], counts)
            seen = jnp.where(mine, 1, seen)
        return chosen, counts

    zero = jnp.zeros((8, 128), jnp.int32)
    chosen, counts = lax.fori_loop(0, groups, pick, (zero, zero))
    pick_v[...] = jnp.where(row == 0, chosen, counts)
    copy = pltpu.make_async_copy(pick_v, pick_s, table_sems.at[1])
    copy.start()
    copy.wait()
    fresh_rows[...] = jnp.zeros_like(fresh_rows)
    factor = 1.0 / math.sqrt(HD)

    def read_query(slot):
        query = queries_v[slot].astype(jnp.float32)
        for g in range(part // 4):
            query_rows[4 * g : 4 * g + 4, :] = query[:, g * HD : (g + 1) * HD]
        fresh_rows[0:4, :] = new_kv_v[slot].astype(jnp.float32)
        return query_rows[...].astype(jnp.bfloat16), fresh_rows[...].astype(jnp.bfloat16)

    def score(query, keys):
        return factor * lax.dot_general(
            query, keys, (((1,), (1,)), ((), ())), preferred_element_type=jnp.float32
        )

    def weigh(weights, values):
        return jnp.dot(weights.astype(jnp.bfloat16), values, preferred_element_type=jnp.float32)

    def store_result(index, rows):
        split_rows(rows, result_rows, results, index)

    def columns_of(scores):
        return lax.broadcasted_iota(jnp.int32, scores.shape, 1)

    def rows_of(scores):
        return lax.broadcasted_iota(jnp.int32, scores.shape, 0)

    def resident(m, carry):
        slot = m
        for k in range(new_count):
            slot = slot + jnp.where(slots_s[k] <= slot, 1, 0)
        query, fresh = read_query(slot)
        pages_read = [resident_v[table_s[j, m]] for j in range(pages_each)]
        cache = jnp.concatenate(pages_read + [fresh], axis=0)
        scores = score(query, cache[:, :HD])
        column = columns_of(scores)
        step = lax.rem(rows_of(scores), 4)
        cached = pages_each * page_size
        bound = jnp.where(column < cached, lengths_s[m], cached + 1 + step)
        scores = jnp.where(column < bound, scores, MASKED)
        largest = jnp.max(scores, axis=1, keepdims=True)
        weights = jnp.exp(scores - largest)
        denominator = jnp.sum(weights, axis=1, keepdims=True)
        store_result(m, weigh(weights, cache[:, HD:]) / denominator)
        return carry

    lax.fori_loop(0, 5, resident, 0)

    chips_arrived(value_rows, 1)

    def pack_values(g, carry):
        for r in range(2):
            page = value_rows[:, send_table_s[r, g]]
            value_send[g, r] = page.reshape(part, HD)
        return carry

    lax.fori_loop(0, groups, pack_values, 0, unroll=2)
    to_groups(value_send, value_recv, 2)

    lax.fori_loop(5, 6, resident, 0)

    groups_arrived(key_recv, 0)

    def turn_keys(p, carry):
        spot = pick_s[0, p]
        page = key_recv[spot // 2, spot % 2]
        for h in range(KV_HEADS):
            key_turn[h, p] = page[h]
        return carry

    lax.fori_loop(0, pages, turn_keys, 0, unroll=4)
    to_chips(lambda h: key_turn.at[h], key_rows, 3)

    lax.fori_loop(6, old_count, resident, 0)

    chips_arrived(key_rows, 3)
    mine = pl.ds(pl.multiple_of(core * part, part), part)

    def place_keys(p, carry):
        arrived[p, mine, :HD] = key_rows[:, p].reshape(part, HD)
        return carry

    lax.fori_loop(0, pages, place_keys, 0, unroll=4)

    def to_sibling(columns, n):
        return pltpu.make_async_remote_copy(
            src_ref=arrived.at[:, mine, columns],
            dst_ref=arrived.at[:, mine, columns],
            send_sem=send_sems.at[n],
            recv_sem=recv_sems.at[n],
            device_id=(me, sibling),
            device_id_type=MESH,
        )

    key_half = to_sibling(pl.ds(0, HD), 4)
    key_half.start()

    key_half.wait()

    def half_of(k, rows, columns):
        first_page = k * pages_each
        return jnp.concatenate(
            [arrived[first_page + j, rows, columns] for j in range(pages_each)], axis=0
        )

    def fresh_scores(k, carry):
        length = 0
        for j in range(pages_each):
            length = length + pick_s[1, k * pages_each + j]
        query, fresh = read_query(slots_s[k])
        scores = []
        for c in range(2):
            keys = half_of(k, pl.ds(c * part, part), pl.ds(0, HD))
            cached = score(query, keys)
            column = columns_of(cached)
            position = column // part * page_size + c * part + column % part
            scores.append(jnp.where(position < length, cached, MASKED))
        own = score(query, fresh[:, :HD])
        scores.append(jnp.where(columns_of(own) <= lax.rem(rows_of(own), 4), own, MASKED))
        largest = functools.reduce(
            jnp.maximum, [jnp.max(x, axis=1, keepdims=True) for x in scores]
        )
        weights = [jnp.exp(x - largest) for x in scores]
        denominator = sum(jnp.sum(x, axis=1, keepdims=True) for x in weights)
        for c in range(2):
            fresh_weights[k, c] = weights[c].astype(jnp.bfloat16)
        fresh_sums[k] = weigh(weights[2], fresh[:, HD:])
        denominators[k] = jnp.broadcast_to(denominator, denominators.shape[1:])
        return carry

    lax.fori_loop(0, new_count, fresh_scores, 0)

    groups_arrived(value_recv, 2)

    def place_values(p, carry):
        spot = pick_s[0, p]
        arrived[p, mine, HD:] = value_recv[spot // 2, spot % 2]
        return carry

    lax.fori_loop(0, pages, place_values, 0, unroll=7)
    value_half = to_sibling(pl.ds(HD, HD), 5)
    value_half.start()

    for k in range(new_count):
        fresh_sums[k] += weigh(fresh_weights[k, core], half_of(k, mine, pl.ds(HD, HD)))

    value_half.wait()

    groups_sent(key_send, 0)
    chips_sent(value_rows, 1)
    groups_sent(value_send, 2)
    chips_sent(key_rows, 3)


def on_device(
    queries,
    new_kv,
    resident_pages,
    arriving_pages,
    block_table,
    old_lengths,
    new_slots,
    page_owner,
    page_position,
    page_tokens,
):
    groups = lax.axis_size("batch")
    pages = arriving_pages.shape[0]
    page_size = resident_pages.shape[1]
    new_count = new_slots.shape[0]
    bf16 = jnp.bfloat16
    dma = pltpu.SemaphoreType.DMA
    half_keys = pages // new_count * page_size // 2
    rows = (new_count, page_size // 2, HD)
    partial = pl.pallas_call(
        exchange_kernel,
        name="exchange_and_attend",
        out_shape=(
            jax.ShapeDtypeStruct((pages,) + resident_pages.shape[1:], bf16),
            jax.ShapeDtypeStruct(block_table.shape[:1] + queries.shape[1:], bf16),
            jax.ShapeDtypeStruct((new_count, 2, page_size // 2, half_keys), bf16),
            jax.ShapeDtypeStruct(rows, jnp.float32),
            jax.ShapeDtypeStruct(rows, jnp.float32),
        ),
        in_specs=[ANY] * 10,
        out_specs=(VMEM,) * 5,
        scratch_shapes=[
            pltpu.VMEM(queries.shape, bf16),
            pltpu.VMEM(new_kv.shape, bf16),
            pltpu.VMEM(resident_pages.shape, bf16),
            pltpu.VMEM(arriving_pages.shape, bf16),
            pltpu.SMEM(block_table.shape[::-1], jnp.int32),
            pltpu.SMEM(old_lengths.shape, jnp.int32),
            pltpu.SMEM(new_slots.shape, jnp.int32),
            pltpu.SMEM(page_owner.shape, jnp.int32),
            pltpu.SMEM(page_position.shape, jnp.int32),
            pltpu.SMEM(page_tokens.shape, jnp.int32),
            pltpu.VMEM((8, 128), jnp.int32),
            pltpu.SMEM((8, 128), jnp.int32),
            pltpu.VMEM((8, 128), jnp.int32),
            pltpu.SMEM((8, 128), jnp.int32),
            pltpu.VMEM((groups, 2, KV_HEADS, 4, HD), bf16),
            pltpu.VMEM((groups, 2, KV_HEADS, 4, HD), bf16),
            pltpu.VMEM((KV_HEADS, pages, 4, HD), bf16),
            pltpu.VMEM((KV_HEADS, pages, 4, HD), bf16),
            pltpu.VMEM((KV_HEADS, pages, 4, HD), bf16),
            pltpu.VMEM((groups, 2, page_size // 2, HD), bf16),
            pltpu.VMEM((groups, 2, page_size // 2, HD), bf16),
            pltpu.VMEM((page_size // 2, HD), jnp.float32),
            pltpu.VMEM((16, 2 * HD), jnp.float32),
            pltpu.VMEM((page_size // 2, HD), jnp.float32),
            dma((10,)),
            dma((2,)),
            dma((6,)),
            dma((6,)),
        ],
        compiler_params=pltpu.CompilerParams(
            collective_id=0, has_side_effects=True, vmem_limit_bytes=48 << 20
        ),
    )(
        *(
            pltpu.with_memory_space_constraint(x, pltpu.HBM)
            for x in (
                queries,
                new_kv,
                resident_pages,
                arriving_pages,
                block_table.T,
                old_lengths,
                new_slots,
                page_owner,
                page_position,
                page_tokens,
            )
        )
    )

    return pl.pallas_call(
        finish_kernel,
        name="finish_fresh",
        out_shape=(
            jax.ShapeDtypeStruct(queries.shape, bf16),
            jax.ShapeDtypeStruct((pages,) + resident_pages.shape[1:], bf16),
        ),
        in_specs=[VMEM] * 5 + [ANY],
        out_specs=(ANY, ANY),
        scratch_shapes=[
            pltpu.SMEM(new_slots.shape, jnp.int32),
            pltpu.VMEM((page_size // 2, HD), jnp.float32),
            pltpu.VMEM((new_count,) + queries.shape[1:], bf16),
            pltpu.VMEM(queries.shape, bf16),
            dma((3,)),
        ],
        compiler_params=pltpu.CompilerParams(vmem_limit_bytes=16 << 20),
    )(*partial, pltpu.with_memory_space_constraint(new_slots, pltpu.HBM))


def solution(mesh):
    return jax.shard_map(
        on_device,
        mesh=mesh,
        in_specs=(
            P("batch", None, "tensor"),
            P("batch", None, "tensor"),
            P("batch", None, "tensor"),
            P("batch", "tensor", None),
            P("batch", None),
            P("batch"),
            P("batch"),
            P(),
            P(),
            P(),
        ),
        out_specs=(P("batch", None, "tensor"), P("batch", None, "tensor")),
        check_vma=False,
    )
```
